32 devices in a mesh: wide: 8 (over z, x), blk: 4 (over y, core).
Axes of the slice: x: 2, y: 2, z: 4, core: 2. Of those that a mesh axis runs over, the one named last changes fastest.
Arguments:
- tokens: bfloat16 [64, 512, 768], P('wide', 'blk'), may hold values from -6 to 6
- lengths: int32 [64, 7], P('wide'), may hold values from 0 to 512, as said below
- query_weight: bfloat16 [768, 768], replicated, may hold values from -0.4375 to 0.4375
- query_bias: bfloat16 [768], replicated, may hold values from -3 to 3
- key_weight: bfloat16 [768, 768], replicated, may hold values from -0.21875 to 0.21875
- value_weight: bfloat16 [768, 768], replicated, may hold values from -0.21875 to 0.21875
- value_bias: bfloat16 [768], replicated, may hold values from -3 to 3
- out_weight: bfloat16 [768, 768], replicated, may hold values from -0.75 to 0.75
- out_bias: bfloat16 [768], replicated, may hold values from -2 to 2
- first_gain: bfloat16 [768], replicated, may hold values from 0.099609375 to 1.8984375
- first_shift: bfloat16 [768], replicated, may hold values from -2 to 2
- inner_weight: bfloat16 [768, 3072], replicated, may hold values from -0.21875 to 0.21875
- inner_bias: bfloat16 [3072], replicated, may hold values from -3 to 3
- outer_weight: bfloat16 [3072, 768], replicated, may hold values from -0.109375 to 0.109375
- outer_bias: bfloat16 [768], replicated, may hold values from -2 to 2
- second_gain: bfloat16 [768], replicated, may hold values from 0.099609375 to 1.8984375
- second_shift: bfloat16 [768], replicated, may hold values from -2 to 2
- cotangent: bfloat16 [64, 512, 768], P('wide', 'blk'), may hold values from -6 to 6
Outputs:
- output: bfloat16 [64, 512, 768], P('wide', 'blk')
- grad_tokens: bfloat16 [64, 512, 768], P('wide', 'blk')
- grad_query_weight: float32 [768, 768], replicated
- grad_query_bias: float32 [768], replicated
- grad_key_weight: float32 [768, 768], replicated
- grad_value_weight: float32 [768, 768], replicated
- grad_value_bias: float32 [768], replicated
- grad_out_weight: float32 [768, 768], replicated
- grad_out_bias: float32 [768], replicated
- grad_first_gain: float32 [768], replicated
- grad_first_shift: float32 [768], replicated
- grad_inner_weight: float32 [768, 3072], replicated
- grad_inner_bias: float32 [3072], replicated
- grad_outer_weight: float32 [3072, 768], replicated
- grad_outer_bias: float32 [768], replicated
- grad_second_gain: float32 [768], replicated
- grad_second_shift: float32 [768], replicated
The draws below stay inside these ranges and needn't reach their ends.
Inputs may be any that keep to these rules, and one draw needn't show every extreme that they name: Each row's 7 lengths sum to 512; entries may be zero; the fourth one is a document that starts within the first 128 tokens of its row and ends within the last 128; some row holds a single document of all 512 tokens.
All inputs are finite; a program needn't handle non-finite values.
Results may differ from the reference program's by a relative error of at most 0.02.
Values may be sent and summed in bfloat16 or wider, within the bound.
No kernel may reach another device: no remote copies, remote signals or barrier semaphores. Data moves between devices by JAX's collectives and lax.ppermute only.
A program may use at most 256 MiB of HBM per device.

```python
import jax
import jax.numpy as jnp
from jax import lax

D = 768
HEADS = 12
HEAD = 64
FF = 3072
ROWS_DEV = 8
TOK_BLK = 128
SEQ = 512
ROWS = 64
N_WIDE = 8
N_BLK = 4


def split_three(key, total):
    cuts = jnp.sort(jax.random.randint(key, (total.shape[0], 2), 0, total[:, None] + 1), axis=-1)
    return jnp.stack([cuts[:, 0], cuts[:, 1] - cuts[:, 0], total - cuts[:, 1]], axis=-1)


def draw_lengths(key, part):
    key = jax.random.fold_in(key, 11)
    keys = jax.random.split(key, 5)
    chosen = jax.random.randint(keys[4], (), 0, ROWS)
    single = jnp.arange(ROWS, dtype=jnp.int32) == chosen
    head = jnp.where(single, 0, jax.random.randint(keys[0], (ROWS,), 0, TOK_BLK))
    tail = jnp.where(single, 0, jax.random.randint(keys[1], (ROWS,), 0, TOK_BLK))
    span = TOK_BLK * N_BLK - head - tail
    return jnp.concatenate([split_three(keys[2], head), span[:, None], split_three(keys[3], tail)], axis=-1).astype(jnp.int32)


def shard_levels(rng, extent, cuts, least, largest):
    def one(dim, shards_of):
        draws = jax.random.uniform(jax.random.fold_in(jax.random.fold_in(rng, 6), dim), (shards_of,), jnp.float32, least / len(cuts), largest / len(cuts))
        return jnp.repeat(jnp.exp(draws), extent[dim] // shards_of).reshape((-1,) + (1,) * (len(extent) - dim - 1))

    factor_of = one(*cuts[0])
    for cut in cuts[1:]:
        factor_of = factor_of * one(*cut)
    return factor_of


def centred(own_key, dims, width, limit, pieces=(), kind=jnp.bfloat16):
    entries = width * jax.random.normal(own_key, dims, jnp.float32)
    if pieces:
        entries = entries * shard_levels(own_key, dims, pieces, -0.22, 0.18)
    return jnp.clip(entries, -limit, limit).astype(kind)


def setup_inputs(seed: int = 0) -> dict:
    seeds = jax.random.split(jax.random.key(seed), 19)
    tokens = centred(seeds[0], (ROWS, SEQ, D), 1.0, 6.0, ((0, 8), (1, 4)))
    lengths = draw_lengths(jax.random.fold_in(seeds[18], 71), 0)
    query_weight = centred(seeds[2], (D, D), (D // 4) ** -0.5, 0.4375)
    query_bias = centred(seeds[3], (D,), 0.5, 3.0)
    key_weight = centred(seeds[4], (D, D), D ** -0.5, 0.21875)
    value_weight = centred(seeds[5], (D, D), D ** -0.5, 0.21875)
    value_bias = centred(seeds[6], (D,), 0.5, 3.0)
    out_weight = centred(seeds[7], (D, D), HEAD ** -0.5, 0.75)
    out_bias = centred(seeds[8], (D,), 0.3, 2.0)
    first_gain = jnp.clip(1.0 + 0.18 * jax.random.normal(seeds[9], (D,), jnp.float32), 0.099609375, 1.8984375).astype(jnp.bfloat16)
    first_shift = centred(seeds[10], (D,), 0.3, 2.0)
    inner_weight = centred(seeds[11], (D, FF), D ** -0.5, 0.21875)
    inner_bias = centred(seeds[12], (FF,), 0.5, 3.0)
    outer_weight = centred(seeds[13], (FF, D), FF ** -0.5, 0.109375)
    outer_bias = centred(seeds[14], (D,), 0.3, 2.0)
    second_gain = jnp.clip(1.0 + 0.18 * jax.random.normal(seeds[15], (D,), jnp.float32), 0.099609375, 1.8984375).astype(jnp.bfloat16)
    second_shift = centred(seeds[16], (D,), 0.3, 2.0)
    cotangent = centred(seeds[17], (ROWS, SEQ, D), 1.0, 6.0, ((0, 8), (1, 4)))
    return {"tokens": tokens, "lengths": lengths, "query_weight": query_weight, "query_bias": query_bias, "key_weight": key_weight, "value_weight": value_weight, "value_bias": value_bias, "out_weight": out_weight, "out_bias": out_bias, "first_gain": first_gain, "first_shift": first_shift, "inner_weight": inner_weight, "inner_bias": inner_bias, "outer_weight": outer_weight, "outer_bias": outer_bias, "second_gain": second_gain, "second_shift": second_shift, "cotangent": cotangent}


@jax.custom_vjp
def low(v):
    return lax.optimization_barrier(v.astype(jnp.bfloat16)).astype(jnp.float32)

@jax.custom_vjp
def low_back(v):
    return v

def low_keep(v):
    return (low(v), None)

def low_pass(kept, grad):
    return (grad,)

def back_keep(v):
    return (v, None)

def back_low(kept, grad):
    return (low(grad),)
low.defvjp(low_keep, low_pass)
low_back.defvjp(back_keep, back_low)

def matmul(left, right):
    return jnp.dot(left, right, precision=lax.Precision.HIGHEST, preferred_element_type=jnp.float32)

def norm_layer(value, gain, shift):
    center = value - lax.optimization_barrier(jnp.mean(value, axis=-1, keepdims=True))
    spread = lax.optimization_barrier(jnp.mean(center * center, axis=-1, keepdims=True))
    return center * lax.rsqrt(spread + 1e-12) * gain + shift

def segment_ids(lengths):
    ends = jnp.cumsum(lengths, axis=-1)
    place = jnp.arange(SEQ, dtype=jnp.int32)
    return lax.optimization_barrier(jnp.sum((place[None, :, None] >= ends[:, None, :]).astype(jnp.int32), axis=-1))

def forward(inputs, params, seg):
    wq, bq, wk, wv, bv, wo, bo, g1, e1, w1, c1, w2, c2, g2, e2 = params
    group = inputs.shape[0]
    flat = inputs.reshape(group * SEQ, D)
    query = low(low_back(matmul(flat, wq) + bq)).reshape(group, SEQ, HEADS, HEAD)
    keys = low(low_back(matmul(flat, wk))).reshape(group, SEQ, HEADS, HEAD)
    values = low(low_back(matmul(flat, wv) + bv)).reshape(group, SEQ, HEADS, HEAD)
    scores = jnp.einsum('gqhd,gkhd->ghqk', query, keys, precision=lax.Precision.HIGHEST) * HEAD ** (-0.5)
    scores = low_back(scores)
    allowed = seg[:, None, :, None] == seg[:, None, None, :]
    scores = jnp.where(allowed, scores, -1e+30)
    probs = low(jax.nn.softmax(scores, axis=-1))
    context = jnp.einsum('ghqk,gkhd->gqhd', probs, values, precision=lax.Precision.HIGHEST)
    context = low(low_back(context.reshape(group * SEQ, D)))
    attn = low_back(matmul(context, wo) + bo)
    first = norm_layer(flat + attn, g1, e1)
    hidden = low_back(matmul(low(first), w1) + c1)
    gelled = low(jax.nn.gelu(hidden, approximate=False))
    mixed = low_back(matmul(gelled, w2) + c2)
    result = norm_layer(first + mixed, g2, e2)
    return result.reshape(group, SEQ, D)

def reference(tokens, lengths, query_weight, query_bias, key_weight, value_weight, value_bias, out_weight, out_bias, first_gain, first_shift, inner_weight, inner_bias, outer_weight, outer_bias, second_gain, second_shift, cotangent):
    params = tuple((item.astype(jnp.float32) for item in (query_weight, query_bias, key_weight, value_weight, value_bias, out_weight, out_bias, first_gain, first_shift, inner_weight, inner_bias, outer_weight, outer_bias, second_gain, second_shift)))
    seg = segment_ids(lengths).reshape(N_WIDE, ROWS_DEV, SEQ)
    inputs = tokens.astype(jnp.float32).reshape(N_WIDE, ROWS_DEV, SEQ, D)
    pulls = cotangent.astype(jnp.float32).reshape(N_WIDE, ROWS_DEV, SEQ, D)

    def step(total, item):
        group_in, group_seg, group_pull = item
        result, puller = jax.vjp(lambda a, b: forward(a, b, group_seg), group_in, params)
        grad_in, grad_params = puller(group_pull)
        total = jax.tree.map(lambda a, b: a + b, total, grad_params)
        return (total, (result.astype(jnp.bfloat16), grad_in.astype(jnp.bfloat16)))
    zeros = tuple((jnp.zeros_like(item) for item in params))
    total, (results, grads_in) = lax.scan(step, zeros, (inputs, seg, pulls))
    output = results.reshape(ROWS, SEQ, D)
    grad_tokens = grads_in.reshape(ROWS, SEQ, D)
    return (output, grad_tokens, total[0], total[1], total[2], total[3], total[4], total[5], total[6], total[7], total[8], total[9], total[10], total[11], total[12], total[13], total[14])
```

```python
import functools

import jax
import jax.numpy as jnp
from jax import lax
from jax.experimental import pallas as pl
from jax.experimental.pallas import tpu as pltpu
from jax.sharding import PartitionSpec as P

HEADS = 12
BIG = 1e30
VMEM_LIMIT = 56 * 1024 * 1024
BF = jnp.bfloat16
F32 = jnp.float32


def swap(value, axis, mask):
    size = lax.axis_size(axis)
    return lax.ppermute(value, axis, [(i, i ^ mask) for i in range(size)])


def matmul(left, right):
    return jnp.dot(left, right, preferred_element_type=F32)


def dot_nt(left, right):
    return lax.dot_general(left, right, (((1,), (1,)), ((), ())), preferred_element_type=F32)


def dot_tn(left, right):
    return lax.dot_general(left, right, (((0,), (0,)), ((), ())), preferred_element_type=F32)


def attn_fwd_kernel(q_ref, k_ref, v_ref, e_ref, f_ref, ctx_ref, qb_ref):
    lane = lax.broadcasted_iota(jnp.int32, (1, 128), 1)
    q = q_ref[0] * BF(0.125)
    k = k_ref[0]
    v = v_ref[0]
    e = e_ref[0]
    f = f_ref[0]
    outs = []
    for h in range(2):
        mine = (lane >= 64) if h else (lane < 64)
        other = 0 if h else 64
        qa = jnp.where(mine, q, e)
        ka = jnp.where(mine, k, f)
        va = jnp.where(mine, v, BF(1.0))
        s = dot_nt(qa, ka)
        high = jnp.max(s, axis=-1, keepdims=True)
        p = jnp.exp(s - high).astype(BF)
        o = matmul(p, va)
        total = o[:, other : other + 1]
        outs.append(o * (1.0 / total))
        lse = high + jnp.log(total)
        hi = lse.astype(BF)
        rest = lse - hi.astype(F32)
        mid = rest.astype(BF)
        low = (rest - mid.astype(F32)).astype(BF)
        qb = jnp.where(lane == other + 8, hi, qa)
        qb = jnp.where(lane == other + 9, mid, qb)
        qb_ref[0, h] = jnp.where(lane == other + 10, low, qb)
    ctx_ref[0] = jnp.where(lane < 64, outs[0], outs[1]).astype(BF)


def attn_bwd_kernel(qb_ref, k_ref, v_ref, f_ref, dctx_ref, ctx_ref, dq_ref, dk_ref, dv_ref):
    lane = lax.broadcasted_iota(jnp.int32, (1, 128), 1)
    k = k_ref[0]
    v = v_ref[0]
    f = f_ref[0]
    dctx = dctx_ref[0]
    prod = dctx.astype(F32) * ctx_ref[0].astype(F32)
    dqs, dks, dvs = [], [], []
    for h in range(2):
        mine = (lane >= 64) if h else (lane < 64)
        other = 0 if h else 64
        delta = jnp.sum(jnp.where(mine, prod, 0.0), axis=-1, keepdims=True)
        hi = delta.astype(BF)
        low = (delta - hi.astype(F32)).astype(BF)
        zero = BF(0.0)
        da = jnp.where(mine, dctx, jnp.where(lane == other, hi, jnp.where(lane == other + 1, low, zero)))
        va = jnp.where(mine, v, jnp.where((lane == other) | (lane == other + 1), BF(-1.0), zero))
        kb = jnp.where(mine, k, f)
        qb = qb_ref[0, h]
        st = dot_nt(kb, qb)
        pt = jnp.exp(st)
        dpt = dot_nt(va, da)
        dst = (pt * dpt).astype(BF)
        dvs.append(matmul(pt.astype(BF), da))
        dks.append(matmul(dst, qb))
        dqs.append(dot_tn(dst, k))
    dq_ref[0] = (jnp.where(lane < 64, dqs[0], dqs[1]) * 0.125).astype(BF)
    dk_ref[0] = jnp.where(lane < 64, dks[0], dks[1]).astype(BF)
    dv_ref[0] = jnp.where(lane < 64, dvs[0], dvs[1]).astype(BF)


def attn_forward(q, k, v, e, f):
    rows, seq, model = q.shape
    pairs = model // 128
    wide = pl.BlockSpec((1, seq, 128), lambda r, p: (r, 0, p))
    mask = pl.BlockSpec((1, seq, 128), lambda r, p: (r, 0, 0))
    return pl.pallas_call(
        attn_fwd_kernel,
        grid=(rows, pairs),
        in_specs=[wide, wide, wide, mask, mask],
        out_specs=[wide, pl.BlockSpec((1, 2, seq, 128), lambda r, p: (r, p, 0, 0))],
        out_shape=[
            jax.ShapeDtypeStruct((rows, seq, model), BF),
            jax.ShapeDtypeStruct((rows, 2 * pairs, seq, 128), BF),
        ],
        compiler_params=pltpu.CompilerParams(vmem_limit_bytes=VMEM_LIMIT),
        cost_estimate=pl.CostEstimate(
            flops=4 * rows * pairs * 2 * seq * seq * 256,
            bytes_accessed=rows * seq * model * 12,
            transcendentals=rows * pairs * 2 * seq * seq,
        ),
        name="attn_fwd",
    )(q, k, v, e, f)


def attn_backward(qb, k, v, f, dctx, ctx):
    rows, seq, model = k.shape
    pairs = model // 128
    wide = pl.BlockSpec((1, seq, 128), lambda r, p: (r, 0, p))
    mask = pl.BlockSpec((1, seq, 128), lambda r, p: (r, 0, 0))
    out = jax.ShapeDtypeStruct((rows, seq, model), BF)
    return pl.pallas_call(
        attn_bwd_kernel,
        grid=(rows, pairs),
        in_specs=[pl.BlockSpec((1, 2, seq, 128), lambda r, p: (r, p, 0, 0)), wide, wide, mask, wide, wide],
        out_specs=[wide, wide, wide],
        out_shape=[out, out, out],
        compiler_params=pltpu.CompilerParams(vmem_limit_bytes=VMEM_LIMIT),
        cost_estimate=pl.CostEstimate(
            flops=10 * rows * pairs * 2 * seq * seq * 256,
            bytes_accessed=rows * seq * model * 18,
            transcendentals=rows * pairs * 2 * seq * seq,
        ),
        name="attn_bwd",
    )(qb, k, v, f, dctx, ctx)


def gelu_pair(x):
    mag = jnp.abs(x)
    bell = jnp.exp(-0.5 * x * x)
    t = 1.0 / (1.0 + 0.23164189 * mag)
    poly = t * (0.127414796 + t * (-0.142248368 + t * (0.7107068705 + t * (-0.7265760135 + t * 0.5307027145))))
    tail = poly * bell
    cdf = jnp.where(x >= 0, 1.0 - tail, tail)
    return x * cdf, cdf + x * (bell * 0.3989422804)


def norm_parts(value):
    center = value - jnp.mean(value, axis=-1, keepdims=True)
    spread = jnp.mean(center * center, axis=-1, keepdims=True)
    inv = lax.rsqrt(spread + 1e-12)
    return center * inv, inv


def norm_back(grad, gain, unit, inv):
    scaled = grad * gain
    mean = jnp.mean(scaled, axis=-1, keepdims=True)
    along = jnp.mean(scaled * unit, axis=-1, keepdims=True)
    return inv * (scaled - mean - unit * along)


def add(a, b):
    return (a.astype(F32) + b.astype(F32)).astype(BF)


def scatter_stages(first):
    wide, blk = lax.axis_size("wide"), lax.axis_size("blk")
    across = [("wide", 1), ("blk", 2)] if first == "x" else [("blk", 2), ("wide", 1)]
    stages = [("blk", 1)] + across + [("wide", 2), ("wide", 4)]
    rest = [("wide", 1 << i) for i in range(3, wide.bit_length() - 1)]
    rest += [("blk", 1 << i) for i in range(2, blk.bit_length() - 1)]
    return stages, rest


def bit_of(axis, mask):
    return jnp.where((lax.axis_index(axis) & mask) != 0, 1, 0)


def reduce_scatter(value, first):
    stages, rest = scatter_stages(first)
    for axis, mask in stages:
        half = value.shape[0] // 2
        bit = bit_of(axis, mask)
        send = lax.dynamic_slice_in_dim(value, (1 - bit) * half, half, 0)
        keep = lax.dynamic_slice_in_dim(value, bit * half, half, 0)
        value = add(keep, swap(send, axis, mask))
    for axis, mask in rest:
        value = add(value, swap(value, axis, mask))
    return value


def gather(value, first):
    stages, _ = scatter_stages(first)
    for axis, mask in reversed(stages):
        value = jnp.concatenate([value, swap(value, axis, mask)], axis=0)
    return value


def place_kernel(me_ref, value_ref, out_ref, *, piece):
    low = me_ref[0] & 3
    for i in range(4):
        at = pl.multiple_of((i ^ low) * piece, 8)
        out_ref[i * piece : (i + 1) * piece, :] = value_ref[pl.ds(at, piece), :].astype(F32)


def place(value, first):
    stages, _ = scatter_stages(first)
    me = jnp.int32(0)
    for axis, mask in stages:
        me = me * 2 + bit_of(axis, mask)
    pieces = 1 << len(stages)
    rows, cols = value.shape
    piece = rows // pieces
    group = 4 * piece
    return pl.pallas_call(
        functools.partial(place_kernel, piece=piece),
        grid_spec=pltpu.PrefetchScalarGridSpec(
            num_scalar_prefetch=1,
            grid=(pieces // 4,),
            in_specs=[pl.BlockSpec((group, cols), lambda i, m: (i ^ (m[0] >> 2), 0))],
            out_specs=pl.BlockSpec((group, cols), lambda i, m: (i, 0)),
        ),
        out_shape=jax.ShapeDtypeStruct((rows, cols), F32),
        compiler_params=pltpu.CompilerParams(vmem_limit_bytes=VMEM_LIMIT),
        cost_estimate=pl.CostEstimate(flops=0, bytes_accessed=rows * cols * 6, transcendentals=0),
        name="place",
    )(me.reshape(1).astype(jnp.int32), value)


def sum_all(value, first):
    return place(gather(reduce_scatter(value, first), first), first)


def butterfly(value):
    for axis in ("blk", "wide"):
        for i in range(lax.axis_size(axis).bit_length() - 1):
            value = value + swap(value, axis, 1 << i)
    return value


def to_rows(value):
    parts = lax.axis_size("blk")
    rows, width, model = value.shape
    own = rows // parts
    me = lax.axis_index("blk")
    got = []
    for j in range(parts):
        piece = lax.dynamic_slice_in_dim(value, (me ^ j) * own, own, 0)
        got.append(swap(piece, "blk", j) if j else piece)
    return jnp.stack(got, axis=1).reshape(own, parts * width, model)


def from_rows(value, width):
    parts = lax.axis_size("blk")
    own, _, model = value.shape
    value = value.reshape(own, parts, width, model)
    me = lax.axis_index("blk")
    out = jnp.zeros((own * parts, width, model), value.dtype)
    for j in range(parts):
        piece = value[:, j]
        got = swap(piece, "blk", j) if j else piece
        out = lax.dynamic_update_slice_in_dim(out, got, (me ^ j) * own, 0)
    return out


def mask_lanes(lengths, own, width):
    parts = lax.axis_size("blk")
    me = lax.axis_index("blk")
    mine = lax.dynamic_slice_in_dim(lengths, me * own, own, 0)
    ends = jnp.cumsum(mine, axis=-1)
    start = (me ^ jnp.arange(parts, dtype=jnp.int32)) * width
    place_of = (start[:, None] + jnp.arange(width, dtype=jnp.int32)[None, :]).reshape(-1)
    seg = jnp.sum((place_of[None, :, None] >= ends[:, None, :]).astype(jnp.int32), axis=-1)
    lane = jnp.arange(128, dtype=jnp.int32) % 64
    same = seg[:, :, None] == lane
    docs = lane < 8
    e = jnp.where(same & docs, 1.0, 0.0).astype(BF)
    f = jnp.where(docs & ~same, -BIG, jnp.where((lane >= 8) & (lane < 11), -1.0, 0.0)).astype(BF)
    return e, f


def per_device(
    tokens,
    lengths,
    query_weight,
    query_bias,
    key_weight,
    value_weight,
    value_bias,
    out_weight,
    out_bias,
    first_gain,
    first_shift,
    inner_weight,
    inner_bias,
    outer_weight,
    outer_bias,
    second_gain,
    second_shift,
    cotangent,
):
    rows_dev, width, model = tokens.shape
    parts = lax.axis_size("blk")
    rows, seq = rows_dev // parts, parts * width
    count = rows * seq
    shape3 = (rows, seq, model)
    f32 = lambda item: item.astype(F32)

    x = to_rows(tokens).reshape(count, model)
    pull = to_rows(cotangent).reshape(count, model)
    e, f = mask_lanes(lengths, rows, width)

    q = (matmul(x, query_weight) + f32(query_bias)).astype(BF)
    k = matmul(x, key_weight).astype(BF)
    v = (matmul(x, value_weight) + f32(value_bias)).astype(BF)
    q, k, v = (item.reshape(shape3) for item in (q, k, v))
    ctx3, qb = attn_forward(q, k, v, e, f)
    ctx = ctx3.reshape(count, model)
    z1 = f32(x) + matmul(ctx, out_weight) + f32(out_bias)
    unit1, inv1 = norm_parts(z1)
    y1 = unit1 * f32(first_gain) + f32(first_shift)
    y1_low = y1.astype(BF)
    hidden = matmul(y1_low, inner_weight) + f32(inner_bias)
    gel, slope = gelu_pair(hidden)
    gel = gel.astype(BF)
    slope = slope.astype(BF)
    z2 = y1 + matmul(gel, outer_weight) + f32(outer_bias)
    unit2, inv2 = norm_parts(z2)
    output = (unit2 * f32(second_gain) + f32(second_shift)).astype(BF)
    output = from_rows(output.reshape(shape3), width)

    g = f32(pull)
    grad_g2 = jnp.sum(g * unit2, axis=0)
    grad_e2 = jnp.sum(g, axis=0)
    dz2 = norm_back(g, f32(second_gain), unit2, inv2)
    dff = dz2.astype(BF)
    grad_w2 = dot_tn(gel, dff).astype(BF)
    grad_c2 = jnp.sum(f32(dff), axis=0)
    dh = (dot_nt(dff, outer_weight) * f32(slope)).astype(BF)
    grad_w1 = dot_tn(y1_low, dh).astype(BF)
    grad_c1 = jnp.sum(f32(dh), axis=0)
    dy1 = dz2 + dot_nt(dh, inner_weight)
    grad_g1 = jnp.sum(dy1 * unit1, axis=0)
    grad_e1 = jnp.sum(dy1, axis=0)
    dz1 = norm_back(dy1, f32(first_gain), unit1, inv1)
    da = dz1.astype(BF)
    grad_wo = dot_tn(ctx, da).astype(BF)
    grad_bo = jnp.sum(f32(da), axis=0)
    dctx = dot_nt(da, out_weight).astype(BF).reshape(shape3)
    dq, dk, dv = attn_backward(qb, k, v, f, dctx, ctx3)
    dq, dk, dv = (item.reshape(count, model) for item in (dq, dk, dv))
    grad_wq = dot_tn(x, dq).astype(BF)
    grad_wk = dot_tn(x, dk).astype(BF)
    grad_wv = dot_tn(x, dv).astype(BF)
    grad_bq = jnp.sum(f32(dq), axis=0)
    grad_bv = jnp.sum(f32(dv), axis=0)
    dx = dz1 + dot_nt(dq, query_weight) + dot_nt(dk, key_weight) + dot_nt(dv, value_weight)
    grad_tokens = from_rows(dx.astype(BF).reshape(shape3), width)

    grad_w2 = sum_all(grad_w2, "x")
    grad_w1 = sum_all(grad_w1, "y")
    grad_wo = sum_all(grad_wo, "x")
    grad_wq = sum_all(grad_wq, "y")
    grad_wk = sum_all(grad_wk, "x")
    grad_wv = sum_all(grad_wv, "y")
    small = (grad_bq, grad_bv, grad_bo, grad_g1, grad_e1, grad_c1, grad_c2, grad_g2, grad_e2)
    joined = butterfly(jnp.concatenate(small))
    cuts = []
    at = 0
    for item in small:
        cuts.append(joined[at : at + item.shape[0]])
        at += item.shape[0]
    grad_bq, grad_bv, grad_bo, grad_g1, grad_e1, grad_c1, grad_c2, grad_g2, grad_e2 = cuts
    return (
        output,
        grad_tokens,
        grad_wq,
        grad_bq,
        grad_wk,
        grad_wv,
        grad_bv,
        grad_wo,
        grad_bo,
        grad_g1,
        grad_e1,
        grad_w1,
        grad_c1,
        grad_w2,
        grad_c2,
        grad_g2,
        grad_e2,
    )


def solution(mesh):
    placed = (P("wide", "blk", None), P("wide", None)) + (P(),) * 15 + (P("wide", "blk", None),)
    return jax.shard_map(
        per_device,
        mesh=mesh,
        in_specs=placed,
        out_specs=(P("wide", "blk", None),) * 2 + (P(),) * 15,
        check_vma=False,
    )
```

```python
import functools

import jax
import jax.numpy as jnp
from jax import lax
from jax.experimental import pallas as pl
from jax.experimental.pallas import tpu as pltpu
from jax.sharding import PartitionSpec as P

BIG = 1e30
VMEM_LIMIT = 60 * 1024 * 1024
BF = jnp.bfloat16
F32 = jnp.float32


def matmul(left, right):
    return jnp.dot(left, right, preferred_element_type=F32)


def dot_nt(left, right):
    return lax.dot_general(left, right, (((1,), (1,)), ((), ())), preferred_element_type=F32)


def dot_tn(left, right):
    return lax.dot_general(left, right, (((0,), (0,)), ((), ())), preferred_element_type=F32)


def gelu_pair(x):
    mag = jnp.abs(x)
    bell = jnp.exp(-0.5 * x * x)
    t = 1.0 / (1.0 + 0.23164189 * mag)
    poly = t * (0.127414796 + t * (-0.142248368 + t * (0.7107068705 + t * (-0.7265760135 + t * 0.5307027145))))
    tail = poly * bell
    cdf = jnp.where(x >= 0, 1.0 - tail, tail)
    return x * cdf, cdf + x * (bell * 0.3989422804)


def norm_parts(value):
    center = value - jnp.mean(value, axis=-1, keepdims=True)
    spread = jnp.mean(center * center, axis=-1, keepdims=True)
    inv = lax.rsqrt(spread + 1e-12)
    return center * inv, inv


def norm_back(grad, gain, unit, inv):
    scaled = grad * gain
    mean = jnp.mean(scaled, axis=-1, keepdims=True)
    along = jnp.mean(scaled * unit, axis=-1, keepdims=True)
    return inv * (scaled - mean - unit * along)


def call(kernel, grid, ins, outs, shapes, scratch=(), scalars=0, flops=0, moved=0, exps=0, name=None, aliases=None):
    return pl.pallas_call(
        kernel,
        grid_spec=pltpu.PrefetchScalarGridSpec(
            num_scalar_prefetch=scalars, grid=grid, in_specs=ins, out_specs=outs, scratch_shapes=list(scratch)
        ),
        out_shape=[jax.ShapeDtypeStruct(s, d) for s, d in shapes],
        compiler_params=pltpu.CompilerParams(vmem_limit_bytes=VMEM_LIMIT),
        cost_estimate=pl.CostEstimate(flops=int(flops), bytes_accessed=int(moved), transcendentals=int(exps)),
        input_output_aliases=aliases or {},
        name=name,
    )


def whole(*shape):
    return pl.BlockSpec(shape, lambda *_: (0,) * len(shape))


def column_sum(value):
    return jnp.sum(value, axis=0, keepdims=True)


def attn_fwd_kernel(
    x_ref, wq_ref, wk_ref, wv_ref, wo_ref, bq_ref, bv_ref, bo_ref, e_ref, f_ref,
    q_out, k_out, v_out, ctx_out, rb_out, p_out, unit_ref, inv_ref,
    q_buf, k_buf, v_buf, ctx_buf, rb_buf, p_buf, sems,
):
    r = pl.program_id(0)
    rows = pl.num_programs(0)
    x = x_ref[0]
    e, f = e_ref[0], f_ref[0]
    model = x.shape[1]
    heads = model // 64
    lo = lax.broadcasted_iota(jnp.int32, (1, 128), 1) < 64
    q = (matmul(x, wq_ref[...]) + bq_ref[...].astype(F32)).astype(BF) * BF(0.125)
    k = matmul(x, wk_ref[...]).astype(BF)
    v = (matmul(x, wv_ref[...]) + bv_ref[...].astype(F32)).astype(BF)

    def send(buf, out, slot, row):
        return pltpu.make_async_copy(buf.at[row], out.at[row], sems.at[row, slot])

    def send_p(row, h):
        return pltpu.make_async_copy(p_buf.at[row, h], p_out.at[row, h], sems.at[row, 5 + h])

    q_buf[r], k_buf[r], v_buf[r] = q, k, v
    send(q_buf, q_out, 0, r).start()
    send(k_buf, k_out, 1, r).start()
    send(v_buf, v_out, 2, r).start()
    for p in range(heads // 2):
        cut = slice(p * 128, (p + 1) * 128)
        qp, kp, vp = q[:, cut], k[:, cut], v[:, cut]
        raw = []
        for h in range(2):
            mine = ~lo if h else lo
            qa = jnp.where(mine, qp, e)
            ka = jnp.where(mine, kp, f)
            va = jnp.where(mine, vp, BF(1.0))
            s = dot_nt(qa, ka)
            w = jnp.exp(s - jnp.max(s, axis=-1, keepdims=True)).astype(BF)
            p_buf[r, 2 * p + h] = w
            send_p(r, 2 * p + h).start()
            raw.append(matmul(w, va))
        total = pltpu.roll(jnp.where(lo, raw[1], raw[0]), 64, 1)
        rb = 1.0 / total
        rb_buf[r, :, cut] = rb
        ctx_buf[r, :, cut] = (jnp.where(lo, raw[0], raw[1]) * rb).astype(BF)
    send(ctx_buf, ctx_out, 3, r).start()
    send(rb_buf, rb_out, 4, r).start()
    z = x.astype(F32) + bo_ref[...].astype(F32) + matmul(ctx_buf[r], wo_ref[...])
    unit, inv = norm_parts(z)
    unit_ref[0] = unit
    inv_ref[0] = jnp.broadcast_to(inv, inv_ref.shape[1:])

    @pl.when(r == rows - 1)
    def _():
        @pl.loop(0, rows)
        def _(row):
            send(q_buf, q_out, 0, row).wait()
            send(k_buf, k_out, 1, row).wait()
            send(v_buf, v_out, 2, row).wait()
            send(ctx_buf, ctx_out, 3, row).wait()
            send(rb_buf, rb_out, 4, row).wait()
            for h in range(heads):
                send_p(row, h).wait()


def attn_forward(x, wq, wk, wv, wo, bq, bv, bo, e, f):
    rows, seq, model = x.shape
    heads = model // 64
    full = pl.BlockSpec((1, seq, model), lambda r: (r, 0, 0))
    mask = pl.BlockSpec((1, seq, 128), lambda r: (r, 0, 0))
    far = pl.BlockSpec(memory_space=pl.ANY)
    big, sq = (rows, seq, model), (rows, heads, seq, seq)
    w, b = whole(model, model), whole(1, model)
    return call(
        attn_fwd_kernel,
        (rows,),
        [full, w, w, w, w, b, b, b, mask, mask],
        [far] * 6 + [full, mask],
        [(big, BF)] * 4 + [(big, F32), (sq, BF), (big, F32), ((rows, seq, 128), F32)],
        [pltpu.VMEM(big, BF)] * 4
        + [pltpu.VMEM(big, F32), pltpu.VMEM(sq, BF), pltpu.SemaphoreType.DMA((rows, 5 + heads))],
        flops=rows * seq * model * (8 * model + 8 * seq),
        moved=rows * seq * (model * 16 + heads * seq * 2) + 8 * model * model,
        exps=rows * heads * seq * seq,
        name="attn_fwd",
    )(x, wq, wk, wv, wo, bq, bv, bo, e, f)


def ffn_fwd_kernel(
    unit_ref, g_ref, w1_ref, c1_ref, w2_ref, c2_ref, g1_ref, e1_ref, g2_ref, e2_ref,
    y1_ref, gel_ref, slope_ref, out_ref, dff_ref, sums_ref, acc, *, chunk,
):
    i = pl.program_id(0)
    count = unit_ref.shape[0]
    g1, e1 = g1_ref[...].astype(F32), e1_ref[...].astype(F32)

    @pl.when(i == 0)
    def _():
        y1 = unit_ref[...] * g1 + e1
        y1_ref[...] = y1.astype(BF)
        acc[...] = y1 + c2_ref[...].astype(F32)

    c1 = c1_ref[...].astype(F32)
    for c in range(0, count, chunk):
        cut = slice(c, c + chunk)
        hidden = matmul(y1_ref[cut], w1_ref[...]) + c1
        gel, slope = gelu_pair(hidden)
        gel = gel.astype(BF)
        gel_ref[cut] = gel
        slope_ref[cut] = slope.astype(BF)
        acc[cut] += matmul(gel, w2_ref[...])

    @pl.when(i == pl.num_programs(0) - 1)
    def _():
        g2, e2 = g2_ref[...].astype(F32), e2_ref[...].astype(F32)

        def body(n, sums):
            cut = pl.ds(pl.multiple_of(n * 128, 128), 128)
            unit, inv = norm_parts(acc[cut])
            out_ref[cut] = (unit * g2 + e2).astype(BF)
            g = g_ref[cut].astype(F32)
            dff = norm_back(g, g2, unit, inv).astype(BF)
            dff_ref[cut] = dff
            return sums[0] + column_sum(g * unit), sums[1] + column_sum(g), sums[2] + column_sum(dff.astype(F32))

        zero = jnp.zeros((1, acc.shape[1]), F32)
        sums = lax.fori_loop(0, count // 128, body, (zero, zero, zero))
        sums_ref[...] = jnp.zeros_like(sums_ref)
        for n in range(3):
            sums_ref[n : n + 1] = sums[n]


def ffn_forward(unit, g, w1, c1, w2, c2, g1, e1, g2, e2, tile=512, chunk=256):
    count, model = unit.shape
    ff = w1.shape[1]
    full, b = whole(count, model), whole(1, model)
    cols = pl.BlockSpec((count, tile), lambda i: (0, i))
    return call(
        functools.partial(ffn_fwd_kernel, chunk=chunk),
        (ff // tile,),
        [
            full, full, pl.BlockSpec((model, tile), lambda i: (0, i)), pl.BlockSpec((1, tile), lambda i: (0, i)),
            pl.BlockSpec((tile, model), lambda i: (i, 0)), b, b, b, b, b,
        ],
        [full, cols, cols, full, full, whole(8, model)],
        [((count, model), BF), ((count, ff), BF), ((count, ff), BF), ((count, model), BF), ((count, model), BF), ((8, model), F32)],
        [pltpu.VMEM((count, model), F32)],
        flops=4 * count * model * ff,
        moved=4 * model * ff + 4 * count * ff + 12 * count * model,
        exps=count * ff,
        name="ffn_fwd",
    )(unit, g, w1, c1, w2, c2, g1, e1, g2, e2)


def grad_w2_kernel(half_ref, gel_ref, dff_ref, out_ref):
    out_ref[...] = dot_tn(gel_ref[...], dff_ref[...]).astype(BF)


def grad_w2_half(which, gel, dff, tile=768):
    count, ff = gel.shape
    model = dff.shape[1]
    half = ff // tile // 2
    return call(
        grad_w2_kernel,
        (half,),
        [pl.BlockSpec((count, tile), lambda i, m: (0, i + half * m[0])), whole(count, model)],
        [pl.BlockSpec((tile, model), lambda i, m: (i, 0))],
        [((ff // 2, model), BF)],
        scalars=1,
        flops=count * model * ff,
        moved=count * ff + ff * model,
        name="grad_w2",
    )(which, gel, dff)[0]


def ffn_bwd_kernel(
    core_ref, dff_ref, w2_ref, slope_ref, w1_ref, ys_ref, yk_ref, send_ref, keep_ref, acc, c1_ref, dh_buf, *, chunk
):
    i = pl.program_id(0)
    count = dff_ref.shape[0]

    @pl.when(i == 0)
    def _():
        acc[...] = dff_ref[...].astype(F32)

    total = None
    for c in range(0, count, chunk):
        cut = slice(c, c + chunk)
        dh = (dot_nt(dff_ref[cut], w2_ref[...]) * slope_ref[cut].astype(F32)).astype(BF)
        dh_buf[cut] = dh
        got = column_sum(dh.astype(F32))
        total = got if total is None else total + got
        acc[cut] += dot_nt(dh, w1_ref[...])
    c1_ref[...] = total
    dh = dh_buf[...]
    send_ref[...] = dot_tn(ys_ref[...], dh).astype(BF)
    keep_ref[...] = dot_tn(yk_ref[...], dh).astype(BF)


def ffn_backward(core, dff, w2, slope, w1, y1, chunk=256, tile=768):
    count, model = dff.shape
    ff = w1.shape[1]
    half = model // 2
    full = whole(count, model)
    out = pl.BlockSpec((half, tile), lambda i, m: (0, i))
    return call(
        functools.partial(ffn_bwd_kernel, chunk=chunk),
        (ff // tile,),
        [
            full, pl.BlockSpec((tile, model), lambda i, m: (i, 0)), pl.BlockSpec((count, tile), lambda i, m: (0, i)),
            pl.BlockSpec((model, tile), lambda i, m: (0, i)),
            pl.BlockSpec((count, half), lambda i, m: (0, 1 - m[0])), pl.BlockSpec((count, half), lambda i, m: (0, m[0])),
        ],
        [out, out, full, pl.BlockSpec((1, tile), lambda i, m: (0, i))],
        [((half, ff), BF)] * 2 + [((count, model), F32), ((1, ff), F32)],
        [pltpu.VMEM((count, tile), BF)],
        scalars=1,
        flops=6 * count * model * ff,
        moved=6 * model * ff + 2 * count * ff + 8 * count * model,
        name="ffn_bwd",
    )(core, dff, w2, slope, w1, y1, y1)


def norm_bwd_kernel(
    core_ref, dy_ref, unit_ref, inv_ref, g1_ref, cs_ref, ck_ref, wo_ref,
    send_ref, keep_ref, dctx_ref, da_ref, sums_ref, acc_s, acc_k,
):
    i = pl.program_id(0)
    dy, unit = dy_ref[...], unit_ref[...]
    da = norm_back(dy, g1_ref[...].astype(F32), unit, inv_ref[:, 0:1]).astype(BF)
    da_ref[...] = da
    dctx_ref[...] = dot_nt(da, wo_ref[...]).astype(BF)

    @pl.when(i == 0)
    def _():
        acc_s[...] = jnp.zeros_like(acc_s)
        acc_k[...] = jnp.zeros_like(acc_k)
        sums_ref[...] = jnp.zeros_like(sums_ref)

    acc_s[...] += dot_tn(cs_ref[...], da)
    acc_k[...] += dot_tn(ck_ref[...], da)
    for n, item in enumerate((dy * unit, dy, da.astype(F32))):
        sums_ref[n : n + 1] += column_sum(item)

    @pl.when(i == pl.num_programs(0) - 1)
    def _():
        for n in range(send_ref.shape[0]):
            cut = slice(n * 256, (n + 1) * 256)
            send_ref[n] = acc_s[:, cut].astype(BF)
            keep_ref[n] = acc_k[:, cut].astype(BF)


def norm_backward(core, dy, unit, inv, g1, ctx, wo, tile=256):
    count, model = dy.shape
    half = model // 2
    part = pl.BlockSpec((tile, model), lambda i, m: (i, 0))
    out = whole(model // 256, half, 256)
    return call(
        norm_bwd_kernel,
        (count // tile,),
        [
            part, part, pl.BlockSpec((tile, 128), lambda i, m: (i, 0)), whole(1, model),
            pl.BlockSpec((tile, half), lambda i, m: (i, 1 - m[0])), pl.BlockSpec((tile, half), lambda i, m: (i, m[0])),
            whole(model, model),
        ],
        [out, out, part, part, whole(8, model)],
        [((model // 256, half, 256), BF)] * 2 + [((count, model), BF)] * 2 + [((8, model), F32)],
        [pltpu.VMEM((half, model), F32)] * 2,
        scalars=1,
        flops=4 * count * model * model,
        moved=16 * count * model + 4 * model * model,
        name="norm_bwd",
    )(core, dy, unit, inv, g1, ctx, ctx, wo)


def attn_bwd_kernel(
    core_ref, p_ref, q_ref, k_ref, v_ref, dctx_ref, ctx_ref, rb_ref, xs_ref, xk_ref, wq_ref, wk_ref, wv_ref, dx_ref,
    *rest,
):
    send_ref, keep_ref, dx_out, sums_ref, acc_s, acc_k = rest[-6:]
    r = pl.program_id(0)
    last = pl.num_programs(0) - 1
    lane = lax.broadcasted_iota(jnp.int32, (1, 128), 1)
    lo = lane < 64
    zero = BF(0.0)
    grads = ([], [], [])
    for p in range(q_ref.shape[2] // 128):
        cut = slice(p * 128, (p + 1) * 128)
        q, k, v = q_ref[0, :, cut], k_ref[0, :, cut], v_ref[0, :, cut]
        scaled = dctx_ref[0, :, cut].astype(F32) * rb_ref[0, :, cut]
        da = scaled.astype(BF)
        prod = scaled * ctx_ref[0, :, cut].astype(F32)
        got = ([], [], [])
        for h in range(2):
            mine = ~lo if h else lo
            other = 0 if h else 64
            delta = jnp.sum(jnp.where(mine, prod, 0.0), axis=-1, keepdims=True)
            hi = delta.astype(BF)
            low = (delta - hi.astype(F32)).astype(BF)
            left = jnp.where(mine, da, jnp.where(lane == other, hi, jnp.where(lane == other + 1, low, zero)))
            right = jnp.where(mine, v, jnp.where((lane == other) | (lane == other + 1), BF(-1.0), zero))
            w = p_ref[0, 2 * p + h]
            ds = (w.astype(F32) * dot_nt(left, right)).astype(BF)
            got[0].append(matmul(ds, k))
            got[1].append(dot_tn(ds, q))
            got[2].append(dot_tn(w, da))
        for n in range(3):
            item = jnp.where(lo, got[n][0], got[n][1])
            grads[n].append((item * 0.125 if n == 0 else item).astype(BF))
    dq, dk, dv = (jnp.concatenate(items, axis=1) for items in grads)
    dx = dx_ref[0].astype(F32)
    dx += dot_nt(dq, wq_ref[...]) + dot_nt(dk, wk_ref[...]) + dot_nt(dv, wv_ref[...])
    dx_out[0] = dx.astype(dx_out.dtype)

    @pl.when(r == 0)
    def _():
        acc_s[...] = jnp.zeros_like(acc_s)
        acc_k[...] = jnp.zeros_like(acc_k)
        sums_ref[...] = jnp.zeros_like(sums_ref)

    for n, item in enumerate((dq, dk, dv)):
        acc_s[n] += dot_tn(xs_ref[0], item)
        acc_k[n] += dot_tn(xk_ref[0], item)
    sums_ref[0:1] += column_sum(dq.astype(F32))
    sums_ref[1:2] += column_sum(dv.astype(F32))

    @pl.when(r == last)
    def _():
        send_ref[...] = acc_s[...].astype(BF)
        keep_ref[...] = acc_k[...].astype(BF)


def attn_backward(core, quad, p, q, k, v, dctx, ctx, rb, x, wq, wk, wv, dx, final, grads):
    rows, seq, model = x.shape
    wide = 256
    half = model // 2
    part = pl.BlockSpec((1, seq, wide), lambda r, m: (r, 0, quad))
    weight = pl.BlockSpec((model, wide), lambda r, m: (0, quad))
    full = pl.BlockSpec((1, seq, model), lambda r, m: (r, 0, 0))
    grad = pl.BlockSpec((3, half, wide), lambda r, m: (quad, 0, 0))
    return call(
        attn_bwd_kernel,
        (rows,),
        [pl.BlockSpec((1, wide // 64, seq, seq), lambda r, m: (r, quad, 0, 0))]
        + [part] * 6
        + [
            pl.BlockSpec((1, seq, half), lambda r, m: (r, 0, 1 - m[0])),
            pl.BlockSpec((1, seq, half), lambda r, m: (r, 0, m[0])),
            weight, weight, weight, full,
        ]
        + [pl.BlockSpec(memory_space=pl.ANY)] * len(grads),
        [grad, grad, full, whole(8, wide)],
        [((3 * model // wide, half, wide), BF)] * 2 + [((rows, seq, model), BF if final else F32), ((8, wide), F32)],
        [pltpu.VMEM((3, half, wide), F32)] * 2,
        scalars=1,
        flops=rows * seq * wide * (12 * model + 16 * seq),
        moved=rows * seq * (wide * 24 + model * 8) + 12 * model * wide,
        name="attn_bwd",
        aliases={14: 0, 15: 1} if grads else None,
    )(core, p, q, k, v, dctx, ctx, rb, x, x, wq, wk, wv, dx, *grads)


def hold(*items):
    return lax.optimization_barrier(items)


def swap(value, axis, mask):
    return lax.ppermute(value, axis, [(i, i ^ mask) for i in range(lax.axis_size(axis))])


def add(*items):
    total = items[0].astype(F32)
    for item in items[1:]:
        total = total + item.astype(F32)
    return total.astype(items[0].dtype)


def swap_by(value, partner):
    wide, blk = lax.axis_size("wide"), lax.axis_size("blk")
    pairs = []
    for i in range(wide * blk):
        w, b = partner(i // blk, i % blk)
        pairs.append((i, w * blk + b))
    return lax.ppermute(value, ("wide", "blk"), pairs)


def side(w, b):
    return w, b ^ 1


def first_hop(w, b):
    return (w, b ^ 2) if b & 1 else (w ^ 1, b)


def second_hop(w, b):
    return (w ^ 1, b) if b & 1 else (w, b ^ 2)


PAIRED = (side, first_hop, second_hop)


def bits_of_device():
    w, b = lax.axis_index("wide"), lax.axis_index("blk")
    core, x, y = b & 1, w & 1, (b >> 1) & 1
    odd = core == 1
    return core, jnp.where(odd, y, x), jnp.where(odd, x, y), (w >> 1) & 3


class Sum:
    stages = 8

    def __init__(self, send, keep):
        self.send, self.value = send, keep
        self.stage = 0
        self.flying = None

    def start(self):
        s = self.stage
        axis = self.value.ndim - 2
        rows = self.value.shape[axis]
        bits = bits_of_device()
        piece = lambda at, size: lax.dynamic_slice_in_dim(self.value, at * size, size, axis)
        hops = [lambda w, b, k=k: (w ^ (2 * k), b) for k in range(1, 4)]
        if s == 0:
            self.flying = [swap_by(self.send, side)]
        elif s < 3:
            self.flying = [swap_by(piece(1 - bits[s], rows // 2), PAIRED[s])]
            self.value = piece(bits[s], rows // 2)
        elif s == 3:
            self.flying = [swap_by(piece(bits[3] ^ k, rows // 4), hops[k - 1]) for k in range(1, 4)]
            self.value = piece(bits[3], rows // 4)
        elif s == 4:
            self.flying = [swap_by(self.value, hop) for hop in hops]
        else:
            self.flying = [swap_by(self.value, PAIRED[7 - s])]

    def spread(self):
        for i in range(3, lax.axis_size("wide").bit_length() - 1):
            self.value = add(self.value, swap(self.value, "wide", 1 << i))

    def finish(self):
        if self.stage < 4:
            self.value = add(self.value, *self.flying)
        elif self.stage < 7:
            self.value = jnp.concatenate([self.value, *self.flying], axis=self.value.ndim - 2)
        else:
            self.value = (self.value, self.flying[0])
        self.flying = None
        self.stage += 1


class SmallSum:
    def __init__(self, value):
        self.value = value
        self.stage = 0
        self.pairs = [(axis, 1 << i) for axis in ("blk", "wide") for i in range(lax.axis_size(axis).bit_length() - 1)]
        self.stages = len(self.pairs)

    def start(self):
        self.flying = [swap(self.value, *self.pairs[self.stage])]

    def finish(self):
        self.value = self.value + self.flying[0]
        self.stage += 1


def step(sums, held, compute=None):
    sums = [item for item in sums if item.stage < item.stages]
    for item in sums:
        item.start()
    flying = [item.flying for item in sums]
    flying, held = hold(flying, compute(*held) if compute else held)
    for item, got in zip(sums, flying):
        item.flying = got
        item.finish()
    return held


def merged(tall, broad):
    tall.spread()
    broad.spread()
    model = tall.value.shape[1]
    parts = [broad.value[:, c : c + model] for c in range(0, broad.value.shape[1], model)]
    both = Sum(None, jnp.concatenate([tall.value] + parts, axis=0))
    both.stage = 4
    return both


def step_keep(item, held, compute):
    item.start()
    flying, (keep, *held) = hold(item.flying, compute(*held))
    item.flying, item.value = flying, keep
    item.finish()
    return (keep, *held)


def place_kernel(me_ref, *refs, takes, piece):
    outs = refs[2 * len(takes) :]
    low = me_ref[3]
    i = pl.program_id(0)
    for turn, when in enumerate((i < 4, i >= 4)):

        @pl.when(when)
        def _(turn=turn):
            for n, cuts in enumerate(takes):
                value_ref = refs[2 * n + turn]
                for out, lead, r, rows, a, b, width in cuts:
                    value = (value_ref[...] if lead is None else value_ref[lead]).astype(F32)
                    for k in range(4):
                        at = pl.multiple_of((k ^ low) * rows, 8)
                        top = k * piece + r
                        outs[out][pl.ds(at, rows), b : b + width] = value[top : top + rows, a : a + width]


def place(pairs, takes, shapes):
    core, first, second, low = bits_of_device()
    me = jnp.stack([core, first * 2 + second, second * 2 + first, low]).astype(jnp.int32)
    group = pairs[0][0].shape[-2] // 4

    def own_at(i, m):
        return jnp.minimum(i, 3) ^ m[1]

    def other_at(i, m):
        return jnp.maximum(i - 4, 0) ^ m[2]

    ins = []
    for own, _ in pairs:
        lead, cols = own.shape[:-2], own.shape[-1]
        for at in (own_at, other_at):
            if lead:
                ins.append(pl.BlockSpec((*lead, group, cols), lambda i, m, at=at: (0, at(i, m), 0)))
            else:
                ins.append(pl.BlockSpec((group, cols), lambda i, m, at=at: (at(i, m), 0)))
    out_at = lambda i, m: (jnp.where(i < 4, m[0] * 4 + i, (1 - m[0]) * 4 + i - 4), 0)
    return call(
        functools.partial(place_kernel, takes=takes, piece=group // 4),
        (8,),
        ins,
        [pl.BlockSpec((rows // 8, cols), out_at) for rows, cols in shapes],
        [(shape, F32) for shape in shapes],
        scalars=1,
        moved=6 * sum(rows * cols for rows, cols in shapes),
        name="place",
    )(me, *[item for pair in pairs for item in pair])


def to_rows(value):
    parts = lax.axis_size("blk")
    rows, width, model = value.shape
    own = rows // parts
    me = lax.axis_index("blk")
    got = []
    for j in range(parts):
        piece = lax.dynamic_slice_in_dim(value, (me ^ j) * own, own, 0)
        got.append(swap(piece, "blk", j) if j else piece)
    return got


def rows_of(got):
    own, width, model = got[0].shape
    return jnp.concatenate(got, axis=1)


def from_rows(value, width):
    return [
        swap(value[:, j * width : (j + 1) * width], "blk", j) if j else value[:, :width]
        for j in range(lax.axis_size("blk"))
    ]


def tokens_of(got):
    own, width, model = got[0].shape
    me = lax.axis_index("blk")
    out = jnp.zeros((own * len(got), width, model), got[0].dtype)
    for j, piece in enumerate(got):
        out = lax.dynamic_update_slice_in_dim(out, piece, (me ^ j) * own, 0)
    return out


def mask_lanes(lengths, own, width):
    parts = lax.axis_size("blk")
    me = lax.axis_index("blk")
    mine = lax.dynamic_slice_in_dim(lengths, me * own, own, 0)
    ends = jnp.cumsum(mine, axis=-1)
    start = (me ^ jnp.arange(parts, dtype=jnp.int32)) * width
    place_of = (start[:, None] + jnp.arange(width, dtype=jnp.int32)[None, :]).reshape(-1)
    seg = jnp.sum((place_of[None, :, None] >= ends[:, None, :]).astype(jnp.int32), axis=-1)
    lane = jnp.arange(128, dtype=jnp.int32) % 64
    same = seg[:, :, None] == lane
    docs = lane < 8
    e = jnp.where(same & docs, 1.0, 0.0).astype(BF)
    f = jnp.where(docs & ~same, -BIG, 0.0).astype(BF)
    return e, f


def per_device(
    tokens,
    lengths,
    query_weight,
    query_bias,
    key_weight,
    value_weight,
    value_bias,
    out_weight,
    out_bias,
    first_gain,
    first_shift,
    inner_weight,
    inner_bias,
    outer_weight,
    outer_bias,
    second_gain,
    second_shift,
    cotangent,
):
    rows_dev, width, model = tokens.shape
    parts = lax.axis_size("blk")
    rows, seq = rows_dev // parts, parts * width
    count = rows * seq
    shape3 = (rows, seq, model)
    flat = lambda item: item.reshape(count, item.shape[-1])
    line = lambda item: item.reshape(1, -1)
    bq, bv, bo, c1, c2 = map(line, (query_bias, value_bias, out_bias, inner_bias, outer_bias))
    g1, e1, g2, e2 = map(line, (first_gain, first_shift, second_gain, second_shift))
    core = (lax.axis_index("blk") & 1).reshape(1).astype(jnp.int32)

    e, f = mask_lanes(lengths, rows, width)
    got, e, f, cotangent = hold(to_rows(tokens), e, f, cotangent)
    x = rows_of(got)
    pull = to_rows(cotangent)
    q, k, v, ctx, rb, p, unit, inv = attn_forward(
        x, query_weight, key_weight, value_weight, out_weight, bq, bv, bo, e, f
    )
    unit, pull = hold(unit, pull)
    y1, gel, slope, output, dff, sums_2 = ffn_forward(
        flat(unit), flat(rows_of(pull)), inner_weight, c1, outer_weight, c2, g1, e1, g2, e2
    )
    send = grad_w2_half(1 - core, gel, dff)
    sum2 = Sum(*hold(send, core))
    keep, output = step_keep(sum2, [output, sum2.value], lambda output, core: (grad_w2_half(core, gel, dff), output))
    back = from_rows(output.reshape(shape3), width)
    send, keep, dy, grad_c1 = step(
        [sum2], [dff], lambda dff: ffn_backward(core, dff, outer_weight, slope, inner_weight, y1)
    )
    sum1 = Sum(send, keep)
    send, keep, dctx, da, sums_1 = step(
        [sum2, sum1], [dy], lambda dy: norm_backward(core, dy, flat(unit), flat(inv), g1, flat(ctx), out_weight)
    )
    sum_o = Sum(send, keep)
    dctx, dx = dctx.reshape(shape3), da.reshape(shape3)
    bias, grads = [], []
    quads = model // 256
    for n in range(quads):
        turn = slice(n, n + 1) if n < quads - 1 else slice(n, None)
        (*grads, dx, got), back[turn] = step(
            [item for item in (sum2, sum1, sum_o) if item.stage < 4],
            [dctx, dx, grads, back[turn]],
            lambda dctx, dx, grads, back: (
                attn_backward(
                    core, n, p, q, k, v, dctx, ctx, rb, x, query_weight, key_weight, value_weight, dx, n == quads - 1, grads
                ),
                back,
            ),
        )
        bias.append(got)
    output = tokens_of(back)
    sum3 = Sum(*grads)
    grad_bq = jnp.concatenate([item[0] for item in bias])
    grad_bv = jnp.concatenate([item[1] for item in bias])
    small = (
        grad_bq, grad_bv, sums_1[2], sums_1[0], sums_1[1], grad_c1[0], sums_2[2], sums_2[0], sums_2[1]
    )
    joined = SmallSum(jnp.concatenate(small))
    both = merged(sum2, sum1)
    both.value, sum3.send, joined.value, dx = hold(both.value, sum3.send, joined.value, dx)
    both.start()
    back = from_rows(dx, width)
    step([sum3, joined, sum_o], [])
    step([sum3, joined], [])
    both.flying, back = step([sum3, joined], [both.flying, back])
    both.finish()
    grad_tokens = tokens_of(back)
    step([sum3, joined, both], [])
    sum3.spread()
    sum_o.spread()
    sum3.value = jnp.concatenate([sum3.value, sum_o.value], axis=0)
    step([sum3, joined, both], [])
    step([sum3, both], [])
    ff = inner_weight.shape[1]
    tall, broad = ff // 32, model // 32
    takes = [(0, None, 0, tall, 0, 0, model)]
    takes += [(1, None, tall + c * broad, broad, 0, c * model, model) for c in range(ff // model)]
    grad_w2, grad_w1 = step(
        [sum3], [both.value], lambda value: place([value], [takes], [(ff, model), (model, ff)])
    )
    step([sum3], [])
    takes = [(n, 3 * c + n, 0, broad, 0, 256 * c, 256) for c in range(quads) for n in range(3)]
    takes += [(3, 3 * quads + c, 0, broad, 0, 256 * c, 256) for c in range(quads)]
    grad_wq, grad_wk, grad_wv, grad_wo = place([sum3.value], [takes], [(model, model)] * 4)
    cuts, at = [], 0
    for item in small:
        cuts.append(joined.value[at : at + item.shape[0]])
        at += item.shape[0]
    grad_bq, grad_bv, grad_bo, grad_g1, grad_e1, grad_c1, grad_c2, grad_g2, grad_e2 = cuts
    return (
        output,
        grad_tokens,
        grad_wq,
        grad_bq,
        grad_wk,
        grad_wv,
        grad_bv,
        grad_wo,
        grad_bo,
        grad_g1,
        grad_e1,
        grad_w1,
        grad_c1,
        grad_w2,
        grad_c2,
        grad_g2,
        grad_e2,
    )


def solution(mesh):
    placed = (P("wide", "blk", None), P("wide", None)) + (P(),) * 15 + (P("wide", "blk", None),)
    return jax.shard_map(
        per_device,
        mesh=mesh,
        in_specs=placed,
        out_specs=(P("wide", "blk", None),) * 2 + (P(),) * 15,
        check_vma=False,
    )
```

```python
import functools

import jax
import jax.numpy as jnp
from jax import lax
from jax.experimental import pallas as pl
from jax.experimental.pallas import tpu as pltpu
from jax.sharding import PartitionSpec as P

BIG = 1e30
VMEM_MIB = {"ffn_bwd": 36, "place": 24}
BF = jnp.bfloat16
F32 = jnp.float32


def matmul(left, right):
    return jnp.dot(left, right, preferred_element_type=F32)


def dot_nt(left, right):
    return lax.dot_general(left, right, (((1,), (1,)), ((), ())), preferred_element_type=F32)


def dot_tn(left, right):
    return lax.dot_general(left, right, (((0,), (0,)), ((), ())), preferred_element_type=F32)


def gelu_pair(x):
    mag = jnp.abs(x)
    bell = jnp.exp(-0.5 * x * x)
    t = 1.0 / (1.0 + 0.23164189 * mag)
    poly = t * (0.127414796 + t * (-0.142248368 + t * (0.7107068705 + t * (-0.7265760135 + t * 0.5307027145))))
    tail = poly * bell
    cdf = jnp.where(x >= 0, 1.0 - tail, tail)
    return x * cdf, cdf + x * (bell * 0.3989422804)


def norm_parts(value):
    center = value - jnp.mean(value, axis=-1, keepdims=True)
    spread = jnp.mean(center * center, axis=-1, keepdims=True)
    inv = lax.rsqrt(spread + 1e-12)
    return center * inv, inv


def norm_back(grad, gain, unit, inv):
    scaled = grad * gain
    mean = jnp.mean(scaled, axis=-1, keepdims=True)
    along = jnp.mean(scaled * unit, axis=-1, keepdims=True)
    return inv * (scaled - mean - unit * along)


def call(kernel, grid, ins, outs, shapes, scratch=(), scalars=0, flops=0, moved=0, exps=0, name=None, aliases=None):
    limit = VMEM_MIB.get(name, 60) * 1024 * 1024
    return pl.pallas_call(
        kernel,
        grid_spec=pltpu.PrefetchScalarGridSpec(
            num_scalar_prefetch=scalars, grid=grid, in_specs=ins, out_specs=outs, scratch_shapes=list(scratch)
        ),
        out_shape=[jax.ShapeDtypeStruct(s, d) for s, d in shapes],
        compiler_params=pltpu.CompilerParams(vmem_limit_bytes=limit),
        cost_estimate=pl.CostEstimate(flops=int(flops), bytes_accessed=int(moved), transcendentals=int(exps)),
        input_output_aliases=aliases or {},
        name=name,
    )


def whole(*shape):
    return pl.BlockSpec(shape, lambda *_: (0,) * len(shape))


def column_sum(value):
    return jnp.sum(value, axis=0, keepdims=True)


def attn_fwd_kernel(*refs, row, pieces):
    parts, refs = refs[:pieces], refs[pieces:]
    wq_ref, wk_ref, wv_ref, wo_ref, bq_ref, bv_ref, bo_ref, e_ref, f_ref = refs[:9]
    x_ref, unit_ref, inv_ref, *outs = refs[-16:-7]
    bufs, sems = refs[-7:-1], refs[-1]
    q_buf, k_buf, v_buf, ctx_buf, rb_buf, p_buf = bufs
    x = jnp.concatenate([part[0] for part in parts], axis=0)
    x_ref[0] = x
    e, f = e_ref[0], f_ref[0]
    heads = x.shape[1] // 64
    lo = lax.broadcasted_iota(jnp.int32, (1, 128), 1) < 64
    q = (matmul(x, wq_ref[...]) + bq_ref[...].astype(F32)).astype(BF) * BF(0.125)
    k = matmul(x, wk_ref[...]).astype(BF)
    v = (matmul(x, wv_ref[...]) + bv_ref[...].astype(F32)).astype(BF)

    def send(n):
        return pltpu.make_async_copy(bufs[n], outs[n].at[row], sems.at[n])

    def send_p(h):
        return pltpu.make_async_copy(p_buf.at[h], outs[5].at[row, h], sems.at[5 + h])

    q_buf[...], k_buf[...], v_buf[...] = q, k, v
    for n in range(3):
        send(n).start()
    for p in range(heads // 2):
        cut = slice(p * 128, (p + 1) * 128)
        qp, kp, vp = q[:, cut], k[:, cut], v[:, cut]
        raw = []
        for h in range(2):
            mine = ~lo if h else lo
            qa = jnp.where(mine, qp, e)
            ka = jnp.where(mine, kp, f)
            va = jnp.where(mine, vp, BF(1.0))
            s = dot_nt(qa, ka)
            w = jnp.exp(s - jnp.max(s, axis=-1, keepdims=True)).astype(BF)
            p_buf[2 * p + h] = w
            send_p(2 * p + h).start()
            raw.append(matmul(w, va))
        total = pltpu.roll(jnp.where(lo, raw[1], raw[0]), 64, 1)
        rb = 1.0 / total
        rb_buf[:, cut] = rb
        ctx_buf[:, cut] = (jnp.where(lo, raw[0], raw[1]) * rb).astype(BF)
    send(3).start()
    send(4).start()
    z = x.astype(F32) + bo_ref[...].astype(F32) + matmul(ctx_buf[...], wo_ref[...])
    unit, inv = norm_parts(z)
    unit_ref[0] = unit
    inv_ref[0] = jnp.broadcast_to(inv, inv_ref.shape[1:])
    for n in range(5):
        send(n).wait()
    for h in range(heads):
        send_p(h).wait()


def attn_forward(parts, row, rows, wq, wk, wv, wo, bq, bv, bo, e, f, before):
    seq, model = parts[0].shape[1] * len(parts), parts[0].shape[2]
    heads = model // 64
    full = pl.BlockSpec((1, seq, model), lambda i: (row, 0, 0))
    mask = pl.BlockSpec((1, seq, 128), lambda i: (row, 0, 0))
    far = pl.BlockSpec(memory_space=pl.ANY)
    big, sq = (rows, seq, model), (rows, heads, seq, seq)
    w, b = whole(model, model), whole(1, model)
    first = len(parts) + 9
    return call(
        functools.partial(attn_fwd_kernel, row=row, pieces=len(parts)),
        (1,),
        [whole(*parts[0].shape)] * len(parts) + [w, w, w, w, b, b, b, mask, mask] + [far] * len(before),
        [full, full, mask] + [far] * 6,
        [(big, BF), (big, F32), ((rows, seq, 128), F32)] + [(big, BF)] * 4 + [(big, F32), (sq, BF)],
        [pltpu.VMEM(big[1:], BF)] * 4
        + [pltpu.VMEM(big[1:], F32), pltpu.VMEM(sq[1:], BF), pltpu.SemaphoreType.DMA((5 + heads,))],
        flops=seq * model * (8 * model + 8 * seq),
        moved=seq * (model * 16 + heads * seq * 2) + 8 * model * model,
        exps=heads * seq * seq,
        name="attn_fwd",
        aliases={first + n: n for n in range(9)} if before else None,
    )(*parts, wq, wk, wv, wo, bq, bv, bo, e, f, *before)


def ffn_fwd_kernel(unit_ref, w1_ref, c1_ref, w2_ref, c2_ref, g1_ref, e1_ref, y1_ref, gel_ref, slope_ref, acc, *, chunk):
    i = pl.program_id(0)
    count = unit_ref.shape[0]

    @pl.when(i == 0)
    def _():
        y1 = unit_ref[...] * g1_ref[...].astype(F32) + e1_ref[...].astype(F32)
        y1_ref[...] = y1.astype(BF)
        acc[...] = y1 + c2_ref[...].astype(F32)

    c1 = c1_ref[...].astype(F32)
    for c in range(0, count, chunk):
        cut = slice(c, c + chunk)
        hidden = matmul(y1_ref[cut], w1_ref[...]) + c1
        gel, slope = gelu_pair(hidden)
        gel = gel.astype(BF)
        gel_ref[cut] = gel
        slope_ref[cut] = slope.astype(BF)
        acc[cut] += matmul(gel, w2_ref[...])


def ffn_forward(unit, w1, c1, w2, c2, g1, e1, tile=768, chunk=256):
    count, model = unit.shape
    ff = w1.shape[1]
    full, b = whole(count, model), whole(1, model)
    cols = pl.BlockSpec((count, tile), lambda i: (0, i))
    return call(
        functools.partial(ffn_fwd_kernel, chunk=chunk),
        (ff // tile,),
        [
            full, pl.BlockSpec((model, tile), lambda i: (0, i)), pl.BlockSpec((1, tile), lambda i: (0, i)),
            pl.BlockSpec((tile, model), lambda i: (i, 0)), b, b, b,
        ],
        [full, cols, cols, full],
        [((count, model), BF), ((count, ff), BF), ((count, ff), BF), ((count, model), F32)],
        flops=4 * count * model * ff,
        moved=4 * model * ff + 4 * count * ff + 12 * count * model,
        exps=count * ff,
        name="ffn_fwd",
    )(unit, w1, c1, w2, c2, g1, e1)


def last_norm_kernel(z_ref, *refs):
    parts = refs[:-5]
    g2_ref, e2_ref, out_ref, dff_ref, sums_ref = refs[-5:]
    i = pl.program_id(0)
    g2 = g2_ref[...].astype(F32)
    rows, width, model = z_ref.shape
    unit, inv = norm_parts(z_ref[...].reshape(rows * width, model))
    out_ref[...] = (unit * g2 + e2_ref[...].astype(F32)).astype(BF).reshape(1, rows, width, model)

    @pl.when(i == 0)
    def _():
        sums_ref[...] = jnp.zeros_like(sums_ref)

    for n, part in enumerate(parts):

        @pl.when(i == n)
        def _(part=part):
            g = part[...].reshape(rows * width, model).astype(F32)
            dff = norm_back(g, g2, unit, inv).astype(BF)
            dff_ref[...] = dff.reshape(rows, width, model)
            for m, item in enumerate((g * unit, g, dff.astype(F32))):
                sums_ref[m : m + 1] += column_sum(item)


def last_norm(z, parts, g2, e2):
    rows, width, model = parts[0].shape
    block = pl.BlockSpec((rows, width, model), lambda i: (0, i, 0))
    return call(
        last_norm_kernel,
        (len(parts),),
        [block] + [whole(rows, width, model)] * len(parts) + [whole(1, model)] * 2,
        [pl.BlockSpec((1, rows, width, model), lambda i: (i, 0, 0, 0)), block, whole(8, model)],
        [((len(parts), rows, width, model), BF), (z.shape, BF), ((8, model), F32)],
        moved=10 * z.size,
        name="last_norm",
    )(z, *parts, g2, e2)


def grad_w2_kernel(half_ref, gel_ref, dff_ref, out_ref):
    out_ref[...] = dot_tn(gel_ref[...], dff_ref[...]).astype(BF)


def grad_w2_half(which, gel, dff, tile=768):
    count, ff = gel.shape
    model = dff.shape[1]
    half = ff // tile // 2
    return call(
        grad_w2_kernel,
        (half,),
        [pl.BlockSpec((count, tile), lambda i, m: (0, i + half * m[0])), whole(count, model)],
        [pl.BlockSpec((tile, model), lambda i, m: (i, 0))],
        [((ff // 2, model), BF)],
        scalars=1,
        flops=count * model * ff,
        moved=count * ff + ff * model,
        name="grad_w2",
    )(which, gel, dff)[0]


def ffn_bwd_kernel(core_ref, dff_ref, w2_ref, slope_ref, w1_ref, ys_ref, yk_ref, start_ref, *rest, chunk):
    send_ref, keep_ref, acc, c1_ref, dh_buf = rest[-5:]
    i = pl.program_id(0)
    count = dff_ref.shape[0]

    @pl.when(i == 0)
    def _():
        acc[...] = start_ref[...].astype(F32)

    total = None
    for c in range(0, count, chunk):
        cut = slice(c, c + chunk)
        dh = (dot_nt(dff_ref[cut], w2_ref[...]) * slope_ref[cut].astype(F32)).astype(BF)
        dh_buf[cut] = dh
        got = column_sum(dh.astype(F32))
        total = got if total is None else total + got
        acc[cut] += dot_nt(dh, w1_ref[...])
    c1_ref[pl.ds(i, 1)] = total
    dh = dh_buf[...]
    send_ref[...] = dot_tn(ys_ref[...], dh).astype(BF)
    keep_ref[...] = dot_tn(yk_ref[...], dh).astype(BF)


def ffn_backward(core, dff, w2, slope, w1, y1, start, grads, part, parts, chunk=256, tile=768):
    count, model = dff.shape
    ff = w1.shape[1]
    half = model // 2
    n = ff // tile // parts
    full = whole(count, model)
    out = pl.BlockSpec((half, tile), lambda i, m: (0, i + n * part))
    return call(
        functools.partial(ffn_bwd_kernel, chunk=chunk),
        (n,),
        [
            full, pl.BlockSpec((tile, model), lambda i, m: (i + n * part, 0)),
            pl.BlockSpec((count, tile), lambda i, m: (0, i + n * part)),
            pl.BlockSpec((model, tile), lambda i, m: (0, i + n * part)),
            pl.BlockSpec((count, half), lambda i, m: (0, 1 - m[0])), pl.BlockSpec((count, half), lambda i, m: (0, m[0])),
            full,
        ]
        + [pl.BlockSpec(memory_space=pl.ANY)] * len(grads),
        [out, out, full, whole(8, tile)],
        [((half, ff), BF)] * 2 + [((count, model), F32), ((8, tile), F32)],
        [pltpu.VMEM((count, tile), BF)],
        scalars=1,
        flops=6 * count * model * ff // parts,
        moved=(6 * model * ff + 2 * count * ff) // parts + 8 * count * model,
        name="ffn_bwd",
        aliases={8: 0, 9: 1} if grads else None,
    )(core, dff, w2, slope, w1, y1, y1, start, *grads)


def norm_bwd_kernel(
    core_ref, dy_ref, unit_ref, inv_ref, g1_ref, cs_ref, ck_ref, wo_ref,
    send_ref, keep_ref, dctx_ref, da_ref, sums_ref, acc_s, acc_k,
):
    i = pl.program_id(0)
    dy, unit = dy_ref[...], unit_ref[...]
    da = norm_back(dy, g1_ref[...].astype(F32), unit, inv_ref[:, 0:1]).astype(BF)
    da_ref[...] = da
    dctx_ref[...] = dot_nt(da, wo_ref[...]).astype(BF)

    @pl.when(i == 0)
    def _():
        acc_s[...] = jnp.zeros_like(acc_s)
        acc_k[...] = jnp.zeros_like(acc_k)
        sums_ref[...] = jnp.zeros_like(sums_ref)

    acc_s[...] += dot_tn(cs_ref[...], da)
    acc_k[...] += dot_tn(ck_ref[...], da)
    for n, item in enumerate((dy * unit, dy, da.astype(F32))):
        sums_ref[n : n + 1] += column_sum(item)

    @pl.when(i == pl.num_programs(0) - 1)
    def _():
        for n in range(send_ref.shape[0]):
            cut = slice(n * 256, (n + 1) * 256)
            send_ref[n] = acc_s[:, cut].astype(BF)
            keep_ref[n] = acc_k[:, cut].astype(BF)


def norm_backward(core, dy, unit, inv, g1, ctx, wo, tile=256):
    count, model = dy.shape
    half = model // 2
    part = pl.BlockSpec((tile, model), lambda i, m: (i, 0))
    out = pl.BlockSpec((model // 256, half, 256), lambda i, m: (0, 0, 0))
    return call(
        norm_bwd_kernel,
        (count // tile,),
        [
            part, part, pl.BlockSpec((tile, 128), lambda i, m: (i, 0)), whole(1, model),
            pl.BlockSpec((tile, half), lambda i, m: (i, 1 - m[0])), pl.BlockSpec((tile, half), lambda i, m: (i, m[0])),
            whole(model, model),
        ],
        [out, out, part, part, whole(8, model)],
        [((4 * model // 256, half, 256), BF)] * 2 + [((count, model), BF)] * 2 + [((8, model), F32)],
        [pltpu.VMEM((half, model), F32)] * 2,
        scalars=1,
        flops=4 * count * model * model,
        moved=16 * count * model + 4 * model * model,
        name="norm_bwd",
    )(core, dy, unit, inv, g1, ctx, ctx, wo)


def attn_bwd_kernel(
    core_ref, p_ref, q_ref, k_ref, v_ref, dctx_ref, ctx_ref, rb_ref, xs_ref, xk_ref, *rest
):
    send_ref, keep_ref, dq_ref, dk_ref, dv_ref, sums_ref, acc_s, acc_k = rest[-8:]
    r = pl.program_id(0)
    last = pl.num_programs(0) - 1
    lane = lax.broadcasted_iota(jnp.int32, (1, 128), 1)
    lo = lane < 64
    zero = BF(0.0)
    grads = ([], [], [])
    for p in range(q_ref.shape[2] // 128):
        cut = slice(p * 128, (p + 1) * 128)
        q, k, v = q_ref[0, :, cut], k_ref[0, :, cut], v_ref[0, :, cut]
        scaled = dctx_ref[0, :, cut].astype(F32) * rb_ref[0, :, cut]
        da = scaled.astype(BF)
        prod = scaled * ctx_ref[0, :, cut].astype(F32)
        got = ([], [], [])
        for h in range(2):
            mine = ~lo if h else lo
            other = 0 if h else 64
            delta = jnp.sum(jnp.where(mine, prod, 0.0), axis=-1, keepdims=True)
            hi = delta.astype(BF)
            low = (delta - hi.astype(F32)).astype(BF)
            left = jnp.where(mine, da, jnp.where(lane == other, hi, jnp.where(lane == other + 1, low, zero)))
            right = jnp.where(mine, v, jnp.where((lane == other) | (lane == other + 1), BF(-1.0), zero))
            w = p_ref[0, 2 * p + h]
            ds = (w.astype(F32) * dot_nt(left, right)).astype(BF)
            got[0].append(matmul(ds, k))
            got[1].append(dot_tn(ds, q))
            got[2].append(dot_tn(w, da))
        for n in range(3):
            item = jnp.where(lo, got[n][0], got[n][1])
            grads[n].append((item * 0.125 if n == 0 else item).astype(BF))

    @pl.when(r == 0)
    def _():
        acc_s[...] = jnp.zeros_like(acc_s)
        acc_k[...] = jnp.zeros_like(acc_k)
        sums_ref[...] = jnp.zeros_like(sums_ref)

    for n, (items, ref) in enumerate(zip(grads, (dq_ref, dk_ref, dv_ref))):
        item = jnp.concatenate(items, axis=1)
        ref[0] = item
        acc_s[n] += dot_tn(xs_ref[0], item)
        acc_k[n] += dot_tn(xk_ref[0], item)
        if n != 1:
            at = n // 2
            sums_ref[at : at + 1] += column_sum(item.astype(F32))

    @pl.when(r == last)
    def _():
        send_ref[...] = acc_s[...].astype(BF)
        keep_ref[...] = acc_k[...].astype(BF)


def attn_backward(core, quad, p, q, k, v, dctx, ctx, rb, x, grads):
    rows, seq, model = x.shape
    wide = 256
    half = model // 2
    part = pl.BlockSpec((1, seq, wide), lambda r, m: (r, 0, quad))
    out = pl.BlockSpec((1, seq, wide), lambda r, m: (r, 0, 0))
    grad = pl.BlockSpec((3, half, wide), lambda r, m: (quad + 1, 0, 0))
    return call(
        attn_bwd_kernel,
        (rows,),
        [pl.BlockSpec((1, wide // 64, seq, seq), lambda r, m: (r, quad, 0, 0))]
        + [part] * 6
        + [
            pl.BlockSpec((1, seq, half), lambda r, m: (r, 0, 1 - m[0])),
            pl.BlockSpec((1, seq, half), lambda r, m: (r, 0, m[0])),
        ]
        + [pl.BlockSpec(memory_space=pl.ANY)] * len(grads),
        [grad, grad, out, out, out, whole(8, wide)],
        [(grads[0].shape, BF)] * 2 + [((rows, seq, wide), BF)] * 3 + [((8, wide), F32)],
        [pltpu.VMEM((3, half, wide), F32)] * 2,
        scalars=1,
        flops=rows * seq * wide * (6 * model + 16 * seq),
        moved=rows * seq * (wide * 30 + model * 2) + 6 * model * wide,
        name="attn_bwd",
        aliases={10: 0, 11: 1},
    )(core, p, q, k, v, dctx, ctx, rb, x, x, *grads)


def dx_kernel(da_ref, wq_ref, wk_ref, wv_ref, *rest):
    out_ref = rest[-1]
    total = da_ref[...].astype(F32)
    rows, width, model = total.shape
    total = total.reshape(rows * width, model)
    for n, w_ref in enumerate((wq_ref, wk_ref, wv_ref)):
        for c in range(model // 256):
            item = rest[3 * c + n][...].reshape(rows * width, 256)
            total += dot_nt(item, w_ref[:, c * 256 : (c + 1) * 256])
    out_ref[0] = total.reshape(rows, width, model).astype(BF)


def grad_x(da, wq, wk, wv, parts, width):
    rows, seq, model = da.shape
    block = lambda cols: pl.BlockSpec((rows, width, cols), lambda j: (0, j, 0))
    return call(
        dx_kernel,
        (seq // width,),
        [block(model)] + [whole(model, model)] * 3 + [block(256)] * len(parts),
        [pl.BlockSpec((1, rows, width, model), lambda j: (j, 0, 0, 0))],
        [((seq // width, rows, width, model), BF)],
        flops=6 * rows * seq * model * model,
        moved=10 * rows * seq * model + 6 * model * model,
        name="grad_x",
    )(da, wq, wk, wv, *parts)[0]


def hold(*items):
    return lax.optimization_barrier(items)


def swap(value, axis, mask):
    return lax.ppermute(value, axis, [(i, i ^ mask) for i in range(lax.axis_size(axis))])


def add(*items):
    if len(items) == 1:
        return items[0]
    total = items[0].astype(F32)
    for item in items[1:]:
        total = total + item.astype(F32)
    return total.astype(items[0].dtype)


def swap_by(value, partner):
    wide, blk = lax.axis_size("wide"), lax.axis_size("blk")
    pairs = []
    for i in range(wide * blk):
        w, b = partner(i // blk, i % blk)
        pairs.append((i, w * blk + b))
    return lax.ppermute(value, ("wide", "blk"), pairs)


def side(w, b):
    return w, b ^ 1


def first_hop(w, b):
    return (w, b ^ 2) if b & 1 else (w ^ 1, b)


def second_hop(w, b):
    return (w ^ 1, b) if b & 1 else (w, b ^ 2)


PAIRED = (side, first_hop, second_hop)


def bits_of_device():
    w, b = lax.axis_index("wide"), lax.axis_index("blk")
    core, x, y = b & 1, w & 1, (b >> 1) & 1
    odd = core == 1
    return core, jnp.where(odd, y, x), jnp.where(odd, x, y), (w >> 1) & 3


class Sum:
    stages = 8

    def __init__(self, send, keep, pairs=False):
        self.send, self.terms = send, [keep]
        self.pairs = pairs
        self.stage = 0
        self.flying = None

    def piece(self, at, size):
        axis = self.terms[0].ndim - 2
        return add(*[lax.dynamic_slice_in_dim(item, at * size, size, axis) for item in self.terms])

    def start(self):
        s = self.stage
        rows = self.terms[0].shape[-2] if s else 0
        bits = bits_of_device()
        hops = [lambda w, b, k=k: (w ^ (2 * k), b) for k in range(1, 4)]
        if s == 0:
            self.flying = [swap_by(self.send, side)]
        elif s < 3:
            self.flying = [swap_by(self.piece(1 - bits[s], rows // 2), PAIRED[s])]
            self.terms = [self.piece(bits[s], rows // 2)]
        elif self.pairs and s < 5:
            self.terms = [add(*self.terms)]
            self.flying = [swap(self.terms[0], "wide", 2 if s == 3 else 4)]
        elif s == 3:
            self.flying = [swap_by(self.piece(bits[3] ^ k, rows // 4), hops[k - 1]) for k in range(1, 4)]
            self.terms = [self.piece(bits[3], rows // 4)]
        elif s == 4:
            self.spread()
            self.flying = [swap_by(self.terms[0], hop) for hop in hops]
        else:
            if self.pairs and s == 5:
                self.spread()
            self.flying = [swap_by(self.terms[0], PAIRED[7 - s])]

    def spread(self):
        value = add(*self.terms)
        for i in range(3, lax.axis_size("wide").bit_length() - 1):
            value = add(value, swap(value, "wide", 1 << i))
        self.terms = [value]

    def finish(self):
        self.terms = self.terms + self.flying
        if (5 if self.pairs else 4) <= self.stage < 7:
            self.terms = [jnp.concatenate(self.terms, axis=self.terms[0].ndim - 2)]
        self.flying = None
        self.stage += 1


class SmallSum:
    def __init__(self, value):
        self.value = value
        self.stage = 0
        self.pairs = [(axis, 1 << i) for axis in ("blk", "wide") for i in range(lax.axis_size(axis).bit_length() - 1)]
        self.stages = len(self.pairs)

    def start(self):
        self.flying = [swap(self.value, *self.pairs[self.stage])]

    def finish(self):
        self.value = self.value + self.flying[0]
        self.stage += 1


def step(sums, held, compute=None):
    sums = [item for item in sums if item.stage < item.stages]
    for item in sums:
        item.start()
    flying = [item.flying for item in sums]
    flying, held = hold(flying, compute(*held) if compute else held)
    for item, got in zip(sums, flying):
        item.flying = got
        item.finish()
    return held


def place_kernel(me_ref, *refs, takes, pieces, ordered):
    outs = refs[2 * len(takes) :]
    low = 0 if ordered else me_ref[3]
    i = pl.program_id(0)
    for turn, when in enumerate((i < 4, i >= 4)):

        @pl.when(when)
        def _(turn=turn):
            for n, cuts in enumerate(takes):
                value_ref = refs[2 * n + turn]
                for out, lead, r, rows, a, b, width in cuts:
                    value = (value_ref[...] if lead is None else value_ref[lead]).astype(F32)
                    for k in range(4):
                        at = k * rows if ordered else pl.multiple_of((k ^ low) * rows, 8)
                        top = k * pieces[n] + r
                        outs[out][pl.ds(at, rows), b : b + width] = value[top : top + rows, a : a + width]


def place(pairs, takes, shapes, ordered=False):
    core, first, second, low = bits_of_device()
    me = jnp.stack([core, first * 2 + second, second * 2 + first, low]).astype(jnp.int32)

    def own_at(i, m):
        return jnp.minimum(i, 3) ^ m[1]

    def other_at(i, m):
        return jnp.maximum(i - 4, 0) ^ m[2]

    ins = []
    for own, _ in pairs:
        lead, group, cols = own.shape[:-2], own.shape[-2] // 4, own.shape[-1]
        for at in (own_at, other_at):
            if lead:
                ins.append(pl.BlockSpec((*lead, group, cols), lambda i, m, at=at: (0, at(i, m), 0)))
            else:
                ins.append(pl.BlockSpec((group, cols), lambda i, m, at=at: (at(i, m), 0)))
    out_at = lambda i, m: (jnp.where(i < 4, m[0] * 4 + i, (1 - m[0]) * 4 + i - 4), 0)
    return call(
        functools.partial(place_kernel, takes=takes, pieces=[own.shape[-2] // 16 for own, _ in pairs], ordered=ordered),
        (8,),
        ins,
        [pl.BlockSpec((rows // 8, cols), out_at) for rows, cols in shapes],
        [(shape, F32) for shape in shapes],
        scalars=1,
        moved=6 * sum(rows * cols for rows, cols in shapes),
        name="place",
    )(me, *[item for pair in pairs for item in pair])


def to_rows(value, first, count):
    parts = lax.axis_size("blk")
    own = value.shape[0] // parts
    me = lax.axis_index("blk")
    got = {}
    for j in reversed(range(parts)):
        piece = lax.dynamic_slice_in_dim(value, (me ^ j) * own + first, count, 0)
        got[j] = swap(piece, "blk", j) if j else piece
    return [got[j] for j in range(parts)]


def send_back(pieces):
    return [swap(pieces[j], "blk", j) if j else pieces[0] for j in range(lax.axis_size("blk"))]


def tokens_of(got):
    own, width, model = got[0].shape
    me = lax.axis_index("blk")
    out = jnp.zeros((own * len(got), width, model), got[0].dtype)
    for j, piece in enumerate(got):
        out = lax.dynamic_update_slice_in_dim(out, piece, (me ^ j) * own, 0)
    return out


def mask_lanes(lengths, own, width):
    parts = lax.axis_size("blk")
    me = lax.axis_index("blk")
    mine = lax.dynamic_slice_in_dim(lengths, me * own, own, 0)
    ends = jnp.cumsum(mine, axis=-1)
    start = (me ^ jnp.arange(parts, dtype=jnp.int32)) * width
    place_of = (start[:, None] + jnp.arange(width, dtype=jnp.int32)[None, :]).reshape(-1)
    seg = jnp.sum((place_of[None, :, None] >= ends[:, None, :]).astype(jnp.int32), axis=-1)
    lane = jnp.arange(128, dtype=jnp.int32) % 64
    same = seg[:, :, None] == lane
    docs = lane < 8
    e = jnp.where(same & docs, 1.0, 0.0).astype(BF)
    f = jnp.where(docs & ~same, -BIG, 0.0).astype(BF)
    return e, f


def per_device(
    tokens,
    lengths,
    query_weight,
    query_bias,
    key_weight,
    value_weight,
    value_bias,
    out_weight,
    out_bias,
    first_gain,
    first_shift,
    inner_weight,
    inner_bias,
    outer_weight,
    outer_bias,
    second_gain,
    second_shift,
    cotangent,
):
    rows_dev, width, model = tokens.shape
    parts = lax.axis_size("blk")
    rows, seq = rows_dev // parts, parts * width
    count = rows * seq
    shape3 = (rows, seq, model)
    flat = lambda item: item.reshape(count, item.shape[-1])
    line = lambda item: item.reshape(1, -1)
    bq, bv, bo, c1, c2 = map(line, (query_bias, value_bias, out_bias, inner_bias, outer_bias))
    g1, e1, g2, e2 = map(line, (first_gain, first_shift, second_gain, second_shift))
    core = (lax.axis_index("blk") & 1).reshape(1).astype(jnp.int32)

    e, f = mask_lanes(lengths, rows, width)
    got, e, f, tokens = hold(to_rows(tokens, 0, 1), e, f, tokens)
    before = []
    for r in range(rows):
        later = to_rows(tokens, r + 1, 1) if r + 1 < rows else to_rows(cotangent, 0, rows)
        before = attn_forward(
            got, r, rows, query_weight, key_weight, value_weight, out_weight, bq, bv, bo, e, f, before
        )
        if r + 1 < rows:
            got, before, cotangent = hold(later, before, cotangent)
    x, unit, inv, q, k, v, ctx, rb, p = before
    y1, gel, slope, z2 = ffn_forward(flat(unit), inner_weight, c1, outer_weight, c2, g1, e1)
    z2, pull = hold(z2, later)
    output, dff, sums_2 = last_norm(z2.reshape(shape3), pull, g2, e2)
    dff = flat(dff)
    back = send_back(output)
    send = grad_w2_half(1 - core, gel, dff)
    sum2 = Sum(*hold(send, core))
    sum2.start()
    sum2.flying, back[:3], keep = hold(sum2.flying, back[:3], grad_w2_half(sum2.terms[0], gel, dff))
    sum2.terms = [keep]
    sum2.finish()
    ff = inner_weight.shape[1]
    dy, grads, grad_c1 = dff, [], []
    for n in range(2):
        *grads, dy, got = step(
            [sum2],
            [dff, dy, grads],
            lambda dff, dy, grads: ffn_backward(
                core, dff, outer_weight, slope, inner_weight, y1, dy, grads, n, 2
            ),
        )
        grad_c1.append(got)
    sum1 = Sum(*grads)
    (*grads, dctx, da, sums_1), back[3:] = step(
        [sum2, sum1],
        [dy, back[3:]],
        lambda dy, back: (norm_backward(core, dy, flat(unit), flat(inv), g1, flat(ctx), out_weight), back),
    )
    output = tokens_of(back)
    dctx = dctx.reshape(shape3)
    bias, grads_x = [], []
    quads = model // 256
    for n in range(quads):
        (*grads, dq, dk, dv, got), output = step(
            [sum2, sum1],
            [dctx, grads, output],
            lambda dctx, grads, output: (attn_backward(core, n, p, q, k, v, dctx, ctx, rb, x, grads), output),
        )
        bias.append(got)
        grads_x += [dq, dk, dv]
    sum3 = Sum(*grads)
    tall, broad = ff // 32, model // 32
    sum1.start()
    bias = jnp.concatenate([item[:2] for item in bias], axis=1)
    small = jnp.concatenate([bias, sums_1[:3], sums_2[:3]] + [item[: ff // model // 2] for item in grad_c1], axis=0)
    sum2.terms, small = step([sum3], [sum2.terms, small])
    joined = SmallSum(small)
    (dx,) = step(
        [sum3, sum2, joined],
        [grads_x],
        lambda parts: [grad_x(da.reshape(shape3), query_weight, key_weight, value_weight, parts, width)],
    )
    back = [dx[0], swap(dx[1], "blk", 1)]
    back, dx = step([sum3, joined], [back, dx])
    (sum1.flying,) = hold(sum1.flying)
    sum1.finish()
    back.append(swap(dx[2], "blk", 2))
    back, dx = step([sum3, sum1], [back, dx])
    back.append(swap(dx[3], "blk", 3))
    (grad_w2,), back = step(
        [sum3, sum1],
        [sum2.terms, back],
        lambda value, back: (place([value], [[(0, None, 0, tall, 0, 0, model)]], [(ff, model)]), back),
    )
    grad_tokens = tokens_of(back)
    grad_tokens, sum1.terms = step([sum3, joined], [grad_tokens, sum1.terms])
    step([sum3, sum1, joined], [])
    (grad_w1,) = step(
        [sum3, joined],
        [sum1.terms],
        lambda value: place([value], [[(0, None, 0, broad, 0, 0, ff)]], [(model, ff)]),
    )
    sums = [joined.value[n] for n in range(8)] + [joined.value[8:].reshape(-1)]
    takes = [(n, 3 + 3 * c + n, 0, broad, 0, 256 * c, 256) for c in range(quads) for n in range(3)]
    takes += [(3, c, 0, broad, 0, 256 * c, 256) for c in range(quads)]
    grad_wq, grad_wk, grad_wv, grad_wo = place([sum3.terms], [takes], [(model, model)] * 4)
    grad_bq, grad_bv, grad_g1, grad_e1, grad_bo, grad_g2, grad_e2, grad_c2, grad_c1 = sums
    return (
        output,
        grad_tokens,
        grad_wq,
        grad_bq,
        grad_wk,
        grad_wv,
        grad_bv,
        grad_wo,
        grad_bo,
        grad_g1,
        grad_e1,
        grad_w1,
        grad_c1,
        grad_w2,
        grad_c2,
        grad_g2,
        grad_e2,
    )


def solution(mesh):
    placed = (P("wide", "blk", None), P("wide", None)) + (P(),) * 15 + (P("wide", "blk", None),)
    return jax.shard_map(
        per_device,
        mesh=mesh,
        in_specs=placed,
        out_specs=(P("wide", "blk", None),) * 2 + (P(),) * 15,
        check_vma=False,
    )
```

```python
import functools

import jax
import jax.numpy as jnp
from jax import lax
from jax.experimental import pallas as pl
from jax.experimental.pallas import tpu as pltpu
from jax.sharding import PartitionSpec as P

BIG = 1e30
VMEM_MIB = {"ffn_bwd": 30, "place": 16, "grad_x": 40}
BF = jnp.bfloat16
F32 = jnp.float32


def matmul(left, right):
    return jnp.dot(left, right, preferred_element_type=F32)


def dot_nt(left, right):
    return lax.dot_general(left, right, (((1,), (1,)), ((), ())), preferred_element_type=F32)


def dot_tn(left, right):
    return lax.dot_general(left, right, (((0,), (0,)), ((), ())), preferred_element_type=F32)


def gelu_pair(x):
    mag = jnp.abs(x)
    bell = jnp.exp(-0.5 * x * x)
    t = 1.0 / (1.0 + 0.23164189 * mag)
    poly = t * (0.127414796 + t * (-0.142248368 + t * (0.7107068705 + t * (-0.7265760135 + t * 0.5307027145))))
    tail = poly * bell
    cdf = jnp.where(x >= 0, 1.0 - tail, tail)
    return x * cdf, cdf + x * (bell * 0.3989422804)


def norm_parts(value):
    center = value - jnp.mean(value, axis=-1, keepdims=True)
    spread = jnp.mean(center * center, axis=-1, keepdims=True)
    inv = lax.rsqrt(spread + 1e-12)
    return center * inv, inv


def norm_back(grad, gain, unit, inv):
    scaled = grad * gain
    mean = jnp.mean(scaled, axis=-1, keepdims=True)
    along = jnp.mean(scaled * unit, axis=-1, keepdims=True)
    return inv * (scaled - mean - unit * along)


def call(kernel, grid, ins, outs, shapes, scratch=(), scalars=0, flops=0, moved=0, exps=0, name=None, aliases=None):
    limit = VMEM_MIB.get(name, 60) * 1024 * 1024
    return pl.pallas_call(
        kernel,
        grid_spec=pltpu.PrefetchScalarGridSpec(
            num_scalar_prefetch=scalars, grid=grid, in_specs=ins, out_specs=outs, scratch_shapes=list(scratch)
        ),
        out_shape=[jax.ShapeDtypeStruct(s, d) for s, d in shapes],
        compiler_params=pltpu.CompilerParams(vmem_limit_bytes=limit),
        cost_estimate=pl.CostEstimate(flops=int(flops), bytes_accessed=int(moved), transcendentals=int(exps)),
        input_output_aliases=aliases or {},
        name=name,
    )


def whole(*shape):
    return pl.BlockSpec(shape, lambda *_: (0,) * len(shape))


def column_sum(value):
    return jnp.sum(value, axis=0, keepdims=True)


def attn_fwd_kernel(*refs, row, pieces):
    parts, refs = refs[:pieces], refs[pieces:]
    wq_ref, wk_ref, wv_ref, wo_ref, bq_ref, bv_ref, bo_ref, e_ref, f_ref = refs[:9]
    x_ref, unit_ref, inv_ref, *outs = refs[-16:-7]
    bufs, sems = refs[-7:-1], refs[-1]
    q_buf, k_buf, v_buf, ctx_buf, rb_buf, p_buf = bufs
    x = jnp.concatenate([part[0] for part in parts], axis=0)
    x_ref[0] = x
    e, f = e_ref[0], f_ref[0]
    heads = x.shape[1] // 64
    lo = lax.broadcasted_iota(jnp.int32, (1, 128), 1) < 64
    q = (matmul(x, wq_ref[...]) + bq_ref[...].astype(F32)).astype(BF) * BF(0.125)
    k = matmul(x, wk_ref[...]).astype(BF)
    v = (matmul(x, wv_ref[...]) + bv_ref[...].astype(F32)).astype(BF)

    def send(n):
        return pltpu.make_async_copy(bufs[n], outs[n].at[row], sems.at[n])

    def send_p(h):
        return pltpu.make_async_copy(p_buf.at[h], outs[5].at[row, h], sems.at[5 + h])

    q_buf[...], k_buf[...], v_buf[...] = q, k, v
    for n in range(3):
        send(n).start()
    for p in range(heads // 2):
        cut = slice(p * 128, (p + 1) * 128)
        qp, kp, vp = q[:, cut], k[:, cut], v[:, cut]
        raw = []
        for h in range(2):
            mine = ~lo if h else lo
            qa = jnp.where(mine, qp, e)
            ka = jnp.where(mine, kp, f)
            va = jnp.where(mine, vp, BF(1.0))
            s = dot_nt(qa, ka)
            w = jnp.exp(s - jnp.max(s, axis=-1, keepdims=True)).astype(BF)
            p_buf[2 * p + h] = w
            send_p(2 * p + h).start()
            raw.append(matmul(w, va))
        total = pltpu.roll(jnp.where(lo, raw[1], raw[0]), 64, 1)
        rb = 1.0 / total
        rb_buf[:, cut] = rb
        ctx_buf[:, cut] = (jnp.where(lo, raw[0], raw[1]) * rb).astype(BF)
    send(3).start()
    send(4).start()
    z = x.astype(F32) + bo_ref[...].astype(F32) + matmul(ctx_buf[...], wo_ref[...])
    unit, inv = norm_parts(z)
    unit_ref[0] = unit
    inv_ref[0] = jnp.broadcast_to(inv, inv_ref.shape[1:])
    for n in range(5):
        send(n).wait()
    for h in range(heads):
        send_p(h).wait()


def attn_forward(parts, row, rows, wq, wk, wv, wo, bq, bv, bo, e, f, before):
    seq, model = parts[0].shape[1] * len(parts), parts[0].shape[2]
    heads = model // 64
    full = pl.BlockSpec((1, seq, model), lambda i: (row, 0, 0))
    mask = pl.BlockSpec((1, seq, 128), lambda i: (row, 0, 0))
    far = pl.BlockSpec(memory_space=pl.ANY)
    big, sq = (rows, seq, model), (rows, heads, seq, seq)
    w, b = whole(model, model), whole(1, model)
    first = len(parts) + 9
    return call(
        functools.partial(attn_fwd_kernel, row=row, pieces=len(parts)),
        (1,),
        [whole(*parts[0].shape)] * len(parts) + [w, w, w, w, b, b, b, mask, mask] + [far] * len(before),
        [full, full, mask] + [far] * 6,
        [(big, BF), (big, F32), ((rows, seq, 128), F32)] + [(big, BF)] * 4 + [(big, F32), (sq, BF)],
        [pltpu.VMEM(big[1:], BF)] * 4
        + [pltpu.VMEM(big[1:], F32), pltpu.VMEM(sq[1:], BF), pltpu.SemaphoreType.DMA((5 + heads,))],
        flops=seq * model * (8 * model + 8 * seq),
        moved=seq * (model * 16 + heads * seq * 2) + 8 * model * model,
        exps=heads * seq * seq,
        name="attn_fwd",
        aliases={first + n: n for n in range(9)} if before else None,
    )(*parts, wq, wk, wv, wo, bq, bv, bo, e, f, *before)


def ffn_fwd_kernel(unit_ref, w1_ref, c1_ref, w2_ref, c2_ref, g1_ref, e1_ref, y1_ref, gel_ref, slope_ref, acc, *, chunk):
    i = pl.program_id(0)
    count = unit_ref.shape[0]

    @pl.when(i == 0)
    def _():
        y1 = unit_ref[...] * g1_ref[...].astype(F32) + e1_ref[...].astype(F32)
        y1_ref[...] = y1.astype(BF)
        acc[...] = y1 + c2_ref[...].astype(F32)

    c1 = c1_ref[...].astype(F32)
    for c in range(0, count, chunk):
        cut = slice(c, c + chunk)
        hidden = matmul(y1_ref[cut], w1_ref[...]) + c1
        gel, slope = gelu_pair(hidden)
        gel = gel.astype(BF)
        gel_ref[cut] = gel
        slope_ref[cut] = slope.astype(BF)
        acc[cut] += matmul(gel, w2_ref[...])


def ffn_forward(unit, w1, c1, w2, c2, g1, e1, tile=768, chunk=256):
    count, model = unit.shape
    ff = w1.shape[1]
    full, b = whole(count, model), whole(1, model)
    cols = pl.BlockSpec((count, tile), lambda i: (0, i))
    return call(
        functools.partial(ffn_fwd_kernel, chunk=chunk),
        (ff // tile,),
        [
            full, pl.BlockSpec((model, tile), lambda i: (0, i)), pl.BlockSpec((1, tile), lambda i: (0, i)),
            pl.BlockSpec((tile, model), lambda i: (i, 0)), b, b, b,
        ],
        [full, cols, cols, full],
        [((count, model), BF), ((count, ff), BF), ((count, ff), BF), ((count, model), F32)],
        flops=4 * count * model * ff,
        moved=4 * model * ff + 4 * count * ff + 12 * count * model,
        exps=count * ff,
        name="ffn_fwd",
    )(unit, w1, c1, w2, c2, g1, e1)


def last_norm_kernel(z_ref, *refs):
    parts = refs[:-5]
    g2_ref, e2_ref, out_ref, dff_ref, sums_ref = refs[-5:]
    i = pl.program_id(0)
    g2 = g2_ref[...].astype(F32)
    rows, width, model = z_ref.shape
    unit, inv = norm_parts(z_ref[...].reshape(rows * width, model))
    out_ref[...] = (unit * g2 + e2_ref[...].astype(F32)).astype(BF).reshape(1, rows, width, model)

    @pl.when(i == 0)
    def _():
        sums_ref[...] = jnp.zeros_like(sums_ref)

    for n, part in enumerate(parts):

        @pl.when(i == n)
        def _(part=part):
            g = part[...].reshape(rows * width, model).astype(F32)
            dff = norm_back(g, g2, unit, inv).astype(BF)
            dff_ref[...] = dff.reshape(rows, width, model)
            for m, item in enumerate((g * unit, g, dff.astype(F32))):
                sums_ref[m : m + 1] += column_sum(item)


def last_norm(z, parts, g2, e2):
    rows, width, model = parts[0].shape
    block = pl.BlockSpec((rows, width, model), lambda i: (0, i, 0))
    return call(
        last_norm_kernel,
        (len(parts),),
        [block] + [whole(rows, width, model)] * len(parts) + [whole(1, model)] * 2,
        [pl.BlockSpec((1, rows, width, model), lambda i: (i, 0, 0, 0)), block, whole(8, model)],
        [((len(parts), rows, width, model), BF), (z.shape, BF), ((8, model), F32)],
        moved=10 * z.size,
        name="last_norm",
    )(z, *parts, g2, e2)


def grad_w2_kernel(half_ref, gel_ref, dff_ref, out_ref):
    out_ref[...] = dot_tn(gel_ref[...], dff_ref[...]).astype(BF)


def grad_w2_half(which, gel, dff, tile=768):
    count, ff = gel.shape
    model = dff.shape[1]
    half = ff // tile // 2
    return call(
        grad_w2_kernel,
        (half,),
        [pl.BlockSpec((count, tile), lambda i, m: (0, i + half * m[0])), whole(count, model)],
        [pl.BlockSpec((tile, model), lambda i, m: (i, 0))],
        [((ff // 2, model), BF)],
        scalars=1,
        flops=count * model * ff,
        moved=count * ff + ff * model,
        name="grad_w2",
    )(which, gel, dff)[0]


def ffn_bwd_kernel(core_ref, dff_ref, w2_ref, slope_ref, w1_ref, ys_ref, yk_ref, start_ref, *rest, chunk):
    send_ref, keep_ref, acc, c1_ref, dh_buf = rest[-5:]
    i = pl.program_id(0)
    count = dff_ref.shape[0]

    @pl.when(i == 0)
    def _():
        acc[...] = start_ref[...].astype(F32)

    total = None
    for c in range(0, count, chunk):
        cut = slice(c, c + chunk)
        dh = (dot_nt(dff_ref[cut], w2_ref[...]) * slope_ref[cut].astype(F32)).astype(BF)
        dh_buf[cut] = dh
        got = column_sum(dh.astype(F32))
        total = got if total is None else total + got
        acc[cut] += dot_nt(dh, w1_ref[...])
    c1_ref[pl.ds(i, 1)] = total
    dh = dh_buf[...]
    send_ref[...] = dot_tn(ys_ref[...], dh).astype(BF)
    keep_ref[...] = dot_tn(yk_ref[...], dh).astype(BF)


def ffn_backward(core, dff, w2, slope, w1, y1, start, grads, part, parts, chunk=256, tile=768):
    count, model = dff.shape
    ff = w1.shape[1]
    half = model // 2
    n = ff // tile // parts
    full = whole(count, model)
    out = pl.BlockSpec((half, tile), lambda i, m: (0, i + n * part))
    return call(
        functools.partial(ffn_bwd_kernel, chunk=chunk),
        (n,),
        [
            full, pl.BlockSpec((tile, model), lambda i, m: (i + n * part, 0)),
            pl.BlockSpec((count, tile), lambda i, m: (0, i + n * part)),
            pl.BlockSpec((model, tile), lambda i, m: (0, i + n * part)),
            pl.BlockSpec((count, half), lambda i, m: (0, 1 - m[0])), pl.BlockSpec((count, half), lambda i, m: (0, m[0])),
            full,
        ]
        + [pl.BlockSpec(memory_space=pl.ANY)] * len(grads),
        [out, out, full, whole(8, tile)],
        [((half, ff), BF)] * 2 + [((count, model), F32), ((8, tile), F32)],
        [pltpu.VMEM((count, tile), BF)],
        scalars=1,
        flops=6 * count * model * ff // parts,
        moved=(6 * model * ff + 2 * count * ff) // parts + 8 * count * model,
        name="ffn_bwd",
        aliases={8: 0, 9: 1} if grads else None,
    )(core, dff, w2, slope, w1, y1, y1, start, *grads)


def norm_bwd_kernel(
    core_ref, dy_ref, unit_ref, inv_ref, g1_ref, cs_ref, ck_ref, wo_ref,
    send_ref, keep_ref, dctx_ref, da_ref, sums_ref, acc_s, acc_k,
):
    i = pl.program_id(0)
    dy, unit = dy_ref[...], unit_ref[...]
    da = norm_back(dy, g1_ref[...].astype(F32), unit, inv_ref[:, 0:1]).astype(BF)
    da_ref[...] = da
    dctx_ref[...] = dot_nt(da, wo_ref[...]).astype(BF)

    @pl.when(i == 0)
    def _():
        acc_s[...] = jnp.zeros_like(acc_s)
        acc_k[...] = jnp.zeros_like(acc_k)
        sums_ref[...] = jnp.zeros_like(sums_ref)

    acc_s[...] += dot_tn(cs_ref[...], da)
    acc_k[...] += dot_tn(ck_ref[...], da)
    for n, item in enumerate((dy * unit, dy, da.astype(F32))):
        sums_ref[n : n + 1] += column_sum(item)

    @pl.when(i == pl.num_programs(0) - 1)
    def _():
        for n in range(send_ref.shape[0]):
            cut = slice(n * 256, (n + 1) * 256)
            send_ref[n] = acc_s[:, cut].astype(BF)
            keep_ref[n] = acc_k[:, cut].astype(BF)


def norm_backward(core, dy, unit, inv, g1, ctx, wo, tile=256):
    count, model = dy.shape
    half = model // 2
    part = pl.BlockSpec((tile, model), lambda i, m: (i, 0))
    out = pl.BlockSpec((model // 256, half, 256), lambda i, m: (0, 0, 0))
    return call(
        norm_bwd_kernel,
        (count // tile,),
        [
            part, part, pl.BlockSpec((tile, 128), lambda i, m: (i, 0)), whole(1, model),
            pl.BlockSpec((tile, half), lambda i, m: (i, 1 - m[0])), pl.BlockSpec((tile, half), lambda i, m: (i, m[0])),
            whole(model, model),
        ],
        [out, out, part, part, whole(8, model)],
        [((4 * model // 256, half, 256), BF)] * 2 + [((count, model), BF)] * 2 + [((8, model), F32)],
        [pltpu.VMEM((half, model), F32)] * 2,
        scalars=1,
        flops=4 * count * model * model,
        moved=16 * count * model + 4 * model * model,
        name="norm_bwd",
    )(core, dy, unit, inv, g1, ctx, ctx, wo)


def attn_bwd_kernel(
    core_ref, p_ref, q_ref, k_ref, v_ref, dctx_ref, ctx_ref, rb_ref, xs_ref, xk_ref, *rest
):
    send_ref, keep_ref, dq_ref, dk_ref, dv_ref, sums_ref, acc_s, acc_k = rest[-8:]
    r = pl.program_id(0)
    last = pl.num_programs(0) - 1
    lane = lax.broadcasted_iota(jnp.int32, (1, 128), 1)
    lo = lane < 64
    zero = BF(0.0)
    grads = ([], [], [])
    for p in range(q_ref.shape[2] // 128):
        cut = slice(p * 128, (p + 1) * 128)
        q, k, v = q_ref[0, :, cut], k_ref[0, :, cut], v_ref[0, :, cut]
        scaled = dctx_ref[0, :, cut].astype(F32) * rb_ref[0, :, cut]
        da = scaled.astype(BF)
        prod = scaled * ctx_ref[0, :, cut].astype(F32)
        got = ([], [], [])
        for h in range(2):
            mine = ~lo if h else lo
            other = 0 if h else 64
            delta = jnp.sum(jnp.where(mine, prod, 0.0), axis=-1, keepdims=True)
            hi = delta.astype(BF)
            low = (delta - hi.astype(F32)).astype(BF)
            left = jnp.where(mine, da, jnp.where(lane == other, hi, jnp.where(lane == other + 1, low, zero)))
            right = jnp.where(mine, v, jnp.where((lane == other) | (lane == other + 1), BF(-1.0), zero))
            w = p_ref[0, 2 * p + h]
            ds = (w.astype(F32) * dot_nt(left, right)).astype(BF)
            got[0].append(matmul(ds, k))
            got[1].append(dot_tn(ds, q))
            got[2].append(dot_tn(w, da))
        for n in range(3):
            item = jnp.where(lo, got[n][0], got[n][1])
            grads[n].append((item * 0.125 if n == 0 else item).astype(BF))

    @pl.when(r == 0)
    def _():
        acc_s[...] = jnp.zeros_like(acc_s)
        acc_k[...] = jnp.zeros_like(acc_k)
        sums_ref[...] = jnp.zeros_like(sums_ref)

    for n, (items, ref) in enumerate(zip(grads, (dq_ref, dk_ref, dv_ref))):
        item = jnp.concatenate(items, axis=1)
        ref[0] = item
        acc_s[n] += dot_tn(xs_ref[0], item)
        acc_k[n] += dot_tn(xk_ref[0], item)
        if n != 1:
            at = n // 2
            sums_ref[at : at + 1] += column_sum(item.astype(F32))

    @pl.when(r == last)
    def _():
        send_ref[...] = acc_s[...].astype(BF)
        keep_ref[...] = acc_k[...].astype(BF)


def attn_backward(core, quad, p, q, k, v, dctx, ctx, rb, x, grads):
    rows, seq, model = x.shape
    wide = 256
    half = model // 2
    part = pl.BlockSpec((1, seq, wide), lambda r, m: (r, 0, quad))
    out = pl.BlockSpec((1, seq, wide), lambda r, m: (r, 0, 0))
    grad = pl.BlockSpec((3, half, wide), lambda r, m: (quad + 1, 0, 0))
    return call(
        attn_bwd_kernel,
        (rows,),
        [pl.BlockSpec((1, wide // 64, seq, seq), lambda r, m: (r, quad, 0, 0))]
        + [part] * 6
        + [
            pl.BlockSpec((1, seq, half), lambda r, m: (r, 0, 1 - m[0])),
            pl.BlockSpec((1, seq, half), lambda r, m: (r, 0, m[0])),
        ]
        + [pl.BlockSpec(memory_space=pl.ANY)] * len(grads),
        [grad, grad, out, out, out, whole(8, wide)],
        [(grads[0].shape, BF)] * 2 + [((rows, seq, wide), BF)] * 3 + [((8, wide), F32)],
        [pltpu.VMEM((3, half, wide), F32)] * 2,
        scalars=1,
        flops=rows * seq * wide * (6 * model + 16 * seq),
        moved=rows * seq * (wide * 30 + model * 2) + 6 * model * wide,
        name="attn_bwd",
        aliases={10: 0, 11: 1},
    )(core, p, q, k, v, dctx, ctx, rb, x, x, *grads)


def dx_kernel(da_ref, wq_ref, wk_ref, wv_ref, *rest):
    out_ref = rest[-1]
    total = da_ref[...].astype(F32)
    rows, width, model = total.shape
    total = total.reshape(rows * width, model)
    for n, w_ref in enumerate((wq_ref, wk_ref, wv_ref)):
        for c in range(model // 256):
            item = rest[3 * c + n][...].reshape(rows * width, 256)
            total += dot_nt(item, w_ref[:, c * 256 : (c + 1) * 256])
    out_ref[0] = total.reshape(rows, width, model).astype(BF)


def grad_x(da, wq, wk, wv, parts, width):
    rows, seq, model = da.shape
    block = lambda cols: pl.BlockSpec((rows, width, cols), lambda j: (0, j, 0))
    return call(
        dx_kernel,
        (seq // width,),
        [block(model)] + [whole(model, model)] * 3 + [block(256)] * len(parts),
        [pl.BlockSpec((1, rows, width, model), lambda j: (j, 0, 0, 0))],
        [((seq // width, rows, width, model), BF)],
        flops=6 * rows * seq * model * model,
        moved=10 * rows * seq * model + 6 * model * model,
        name="grad_x",
    )(da, wq, wk, wv, *parts)[0]


def hold(*items):
    return lax.optimization_barrier(items)


def swap(value, axis, mask):
    return lax.ppermute(value, axis, [(i, i ^ mask) for i in range(lax.axis_size(axis))])


def add(*items):
    if len(items) == 1:
        return items[0]
    total = items[0].astype(F32)
    for item in items[1:]:
        total = total + item.astype(F32)
    return total.astype(items[0].dtype)


def swap_by(value, partner):
    wide, blk = lax.axis_size("wide"), lax.axis_size("blk")
    pairs = []
    for i in range(wide * blk):
        w, b = partner(i // blk, i % blk)
        pairs.append((i, w * blk + b))
    return lax.ppermute(value, ("wide", "blk"), pairs)


def side(w, b):
    return w, b ^ 1


def first_hop(w, b):
    return (w, b ^ 2) if b & 1 else (w ^ 1, b)


def second_hop(w, b):
    return (w ^ 1, b) if b & 1 else (w, b ^ 2)


PAIRED = (side, first_hop, second_hop)


def bits_of_device():
    w, b = lax.axis_index("wide"), lax.axis_index("blk")
    core, x, y = b & 1, w & 1, (b >> 1) & 1
    odd = core == 1
    return core, jnp.where(odd, y, x), jnp.where(odd, x, y), (w >> 1) & 3


class Sum:
    stages = 8

    def __init__(self, send, keep, pairs=False):
        self.send, self.terms = send, [keep]
        self.pairs = pairs
        self.stage = 0
        self.flying = None

    def piece(self, at, size):
        axis = self.terms[0].ndim - 2
        return add(*[lax.dynamic_slice_in_dim(item, at * size, size, axis) for item in self.terms])

    def start(self):
        s = self.stage
        rows = self.terms[0].shape[-2] if s else 0
        bits = bits_of_device()
        hops = [lambda w, b, k=k: (w ^ (2 * k), b) for k in range(1, 4)]
        if s == 0:
            self.flying = [swap_by(self.send, side)]
        elif s < 3:
            self.flying = [swap_by(self.piece(1 - bits[s], rows // 2), PAIRED[s])]
            self.terms = [self.piece(bits[s], rows // 2)]
        elif self.pairs and s < 5:
            self.terms = [add(*self.terms)]
            self.flying = [swap(self.terms[0], "wide", 2 if s == 3 else 4)]
        elif s == 3:
            self.flying = [swap_by(self.piece(bits[3] ^ k, rows // 4), hops[k - 1]) for k in range(1, 4)]
            self.terms = [self.piece(bits[3], rows // 4)]
        elif s == 4:
            self.spread()
            self.flying = [swap_by(self.terms[0], hop) for hop in hops]
        else:
            if self.pairs and s == 5:
                self.spread()
            self.flying = [swap_by(self.terms[0], PAIRED[7 - s])]

    def spread(self):
        value = add(*self.terms)
        for i in range(3, lax.axis_size("wide").bit_length() - 1):
            value = add(value, swap(value, "wide", 1 << i))
        self.terms = [value]

    def finish(self):
        self.terms = self.terms + self.flying
        if (5 if self.pairs else 4) <= self.stage < 7:
            self.terms = [jnp.concatenate(self.terms, axis=self.terms[0].ndim - 2)]
        self.flying = None
        self.stage += 1


class SmallSum:
    def __init__(self, value):
        self.value = value
        self.stage = 0
        self.pairs = [(axis, 1 << i) for axis in ("blk", "wide") for i in range(lax.axis_size(axis).bit_length() - 1)]
        self.stages = len(self.pairs)

    def start(self):
        self.flying = [swap(self.value, *self.pairs[self.stage])]

    def finish(self):
        self.value = self.value + self.flying[0]
        self.stage += 1


def step(sums, held, compute=None):
    sums = [item for item in sums if item.stage < item.stages]
    for item in sums:
        item.start()
    flying = [item.flying for item in sums]
    flying, held = hold(flying, compute(*held) if compute else held)
    for item, got in zip(sums, flying):
        item.flying = got
        item.finish()
    return held


def place_kernel(me_ref, *refs, takes, pieces, ordered):
    outs = refs[2 * len(takes) :]
    low = 0 if ordered else me_ref[3]
    i = pl.program_id(0)
    for turn, when in enumerate((i < 4, i >= 4)):

        @pl.when(when)
        def _(turn=turn):
            for n, cuts in enumerate(takes):
                value_ref = refs[2 * n + turn]
                for out, lead, r, rows, a, b, width in cuts:
                    value = (value_ref[...] if lead is None else value_ref[lead]).astype(F32)
                    for k in range(4):
                        at = k * rows if ordered else pl.multiple_of((k ^ low) * rows, 8)
                        top = k * pieces[n] + r
                        outs[out][pl.ds(at, rows), b : b + width] = value[top : top + rows, a : a + width]


def place(pairs, takes, shapes, ordered=False):
    core, first, second, low = bits_of_device()
    me = jnp.stack([core, first * 2 + second, second * 2 + first, low]).astype(jnp.int32)

    def own_at(i, m):
        return jnp.minimum(i, 3) ^ m[1]

    def other_at(i, m):
        return jnp.maximum(i - 4, 0) ^ m[2]

    ins = []
    for own, _ in pairs:
        lead, group, cols = own.shape[:-2], own.shape[-2] // 4, own.shape[-1]
        for at in (own_at, other_at):
            if lead:
                ins.append(pl.BlockSpec((*lead, group, cols), lambda i, m, at=at: (0, at(i, m), 0)))
            else:
                ins.append(pl.BlockSpec((group, cols), lambda i, m, at=at: (at(i, m), 0)))
    out_at = lambda i, m: (jnp.where(i < 4, m[0] * 4 + i, (1 - m[0]) * 4 + i - 4), 0)
    return call(
        functools.partial(place_kernel, takes=takes, pieces=[own.shape[-2] // 16 for own, _ in pairs], ordered=ordered),
        (8,),
        ins,
        [pl.BlockSpec((rows // 8, cols), out_at) for rows, cols in shapes],
        [(shape, F32) for shape in shapes],
        scalars=1,
        moved=6 * sum(rows * cols for rows, cols in shapes),
        name="place",
    )(me, *[item for pair in pairs for item in pair])


def to_rows(value, first, count):
    parts = lax.axis_size("blk")
    own = value.shape[0] // parts
    me = lax.axis_index("blk")
    got = {}
    for j in reversed(range(parts)):
        piece = lax.dynamic_slice_in_dim(value, (me ^ j) * own + first, count, 0)
        got[j] = swap(piece, "blk", j) if j else piece
    return [got[j] for j in range(parts)]


def send_back(pieces):
    return [swap(pieces[j], "blk", j) if j else pieces[0] for j in range(lax.axis_size("blk"))]


def tokens_of(got):
    own, width, model = got[0].shape
    me = lax.axis_index("blk")
    out = jnp.zeros((own * len(got), width, model), got[0].dtype)
    for j, piece in enumerate(got):
        out = lax.dynamic_update_slice_in_dim(out, piece, (me ^ j) * own, 0)
    return out


def mask_lanes(lengths, own, width):
    parts = lax.axis_size("blk")
    me = lax.axis_index("blk")
    mine = lax.dynamic_slice_in_dim(lengths, me * own, own, 0)
    ends = jnp.cumsum(mine, axis=-1)
    start = (me ^ jnp.arange(parts, dtype=jnp.int32)) * width
    place_of = (start[:, None] + jnp.arange(width, dtype=jnp.int32)[None, :]).reshape(-1)
    seg = jnp.sum((place_of[None, :, None] >= ends[:, None, :]).astype(jnp.int32), axis=-1)
    lane = jnp.arange(128, dtype=jnp.int32) % 64
    same = seg[:, :, None] == lane
    docs = lane < 8
    e = jnp.where(same & docs, 1.0, 0.0).astype(BF)
    f = jnp.where(docs & ~same, -BIG, 0.0).astype(BF)
    return e, f


def per_device(
    tokens,
    lengths,
    query_weight,
    query_bias,
    key_weight,
    value_weight,
    value_bias,
    out_weight,
    out_bias,
    first_gain,
    first_shift,
    inner_weight,
    inner_bias,
    outer_weight,
    outer_bias,
    second_gain,
    second_shift,
    cotangent,
):
    rows_dev, width, model = tokens.shape
    parts = lax.axis_size("blk")
    rows, seq = rows_dev // parts, parts * width
    count = rows * seq
    shape3 = (rows, seq, model)
    flat = lambda item: item.reshape(count, item.shape[-1])
    line = lambda item: item.reshape(1, -1)
    bq, bv, bo, c1, c2 = map(line, (query_bias, value_bias, out_bias, inner_bias, outer_bias))
    g1, e1, g2, e2 = map(line, (first_gain, first_shift, second_gain, second_shift))
    core = (lax.axis_index("blk") & 1).reshape(1).astype(jnp.int32)

    e, f = mask_lanes(lengths, rows, width)
    got, e, f, tokens = hold(to_rows(tokens, 0, 1), e, f, tokens)
    before = []
    for r in range(rows):
        later = to_rows(tokens, r + 1, 1) if r + 1 < rows else to_rows(cotangent, 0, rows)
        before = attn_forward(
            got, r, rows, query_weight, key_weight, value_weight, out_weight, bq, bv, bo, e, f, before
        )
        if r + 1 < rows:
            got, before, cotangent = hold(later, before, cotangent)
    x, unit, inv, q, k, v, ctx, rb, p = before
    y1, gel, slope, z2 = ffn_forward(flat(unit), inner_weight, c1, outer_weight, c2, g1, e1)
    z2, pull = hold(z2, later)
    output, dff, sums_2 = last_norm(z2.reshape(shape3), pull, g2, e2)
    dff = flat(dff)
    back = send_back(output)
    send = grad_w2_half(1 - core, gel, dff)
    sum2 = Sum(*hold(send, core))
    sum2.start()
    sum2.flying, back[:3], keep = hold(sum2.flying, back[:3], grad_w2_half(sum2.terms[0], gel, dff))
    sum2.terms = [keep]
    sum2.finish()
    ff = inner_weight.shape[1]
    dy, grads, grad_c1 = dff, [], []
    for n in range(2):
        *grads, dy, got = step(
            [sum2],
            [dff, dy, grads],
            lambda dff, dy, grads: ffn_backward(
                core, dff, outer_weight, slope, inner_weight, y1, dy, grads, n, 2
            ),
        )
        grad_c1.append(got)
    sum1 = Sum(*grads)
    (*grads, dctx, da, sums_1), back[3:] = step(
        [sum2, sum1],
        [dy, back[3:]],
        lambda dy, back: (norm_backward(core, dy, flat(unit), flat(inv), g1, flat(ctx), out_weight), back),
    )
    output = tokens_of(back)
    dctx = dctx.reshape(shape3)
    bias, grads_x = [], []
    quads = model // 256
    for n in range(quads):
        (*grads, dq, dk, dv, got), output = step(
            [sum2, sum1],
            [dctx, grads, output],
            lambda dctx, grads, output: (attn_backward(core, n, p, q, k, v, dctx, ctx, rb, x, grads), output),
        )
        bias.append(got)
        grads_x += [dq, dk, dv]
    sum3 = Sum(*grads)
    tall, broad = ff // 32, model // 32
    sum1.start()
    bias = jnp.concatenate([item[:2] for item in bias], axis=1)
    small = jnp.concatenate([bias, sums_1[:3], sums_2[:3]] + [item[: ff // model // 2] for item in grad_c1], axis=0)
    sum2.terms, small = step([sum3], [sum2.terms, small])
    joined = SmallSum(small)
    (dx,) = step(
        [sum3, sum2, joined],
        [grads_x],
        lambda parts: [grad_x(da.reshape(shape3), query_weight, key_weight, value_weight, parts, width)],
    )
    back = [dx[0], swap(dx[1], "blk", 1)]
    back, dx = step([sum3, joined], [back, dx])
    (sum1.flying,) = hold(sum1.flying)
    sum1.finish()
    back.append(swap(dx[2], "blk", 2))
    back, dx = step([sum3, sum1], [back, dx])
    back.append(swap(dx[3], "blk", 3))
    (grad_w2,), back = step(
        [sum3, sum1],
        [sum2.terms, back],
        lambda value, back: (place([value], [[(0, None, 0, tall, 0, 0, model)]], [(ff, model)]), back),
    )
    grad_tokens = tokens_of(back)
    grad_tokens, sum1.terms = step([sum3, joined], [grad_tokens, sum1.terms])
    step([sum3, sum1, joined], [])
    grad_w1, joined.value = step(
        [sum3],
        [sum1.terms, joined.value],
        lambda value, small: (place([value], [[(0, None, 0, broad, 0, 0, ff)]], [(model, ff)])[0], small),
    )
    takes = [(n, 3 + 3 * c + n, 0, broad, 0, 256 * c, 256) for c in range(quads) for n in range(3)]
    takes += [(3, c, 0, broad, 0, 256 * c, 256) for c in range(quads)]
    grad_wq, grad_wk, grad_wv, grad_wo = step(
        [joined], [sum3.terms], lambda value: place([value], [takes], [(model, model)] * 4)
    )
    grad_bq, grad_bv, grad_g1, grad_e1, grad_bo, grad_g2, grad_e2, grad_c2 = [joined.value[n] for n in range(8)]
    grad_c1 = joined.value[8:].reshape(-1)
    return (
        output,
        grad_tokens,
        grad_wq,
        grad_bq,
        grad_wk,
        grad_wv,
        grad_bv,
        grad_wo,
        grad_bo,
        grad_g1,
        grad_e1,
        grad_w1,
        grad_c1,
        grad_w2,
        grad_c2,
        grad_g2,
        grad_e2,
    )


def solution(mesh):
    placed = (P("wide", "blk", None), P("wide", None)) + (P(),) * 15 + (P("wide", "blk", None),)
    return jax.shard_map(
        per_device,
        mesh=mesh,
        in_specs=placed,
        out_specs=(P("wide", "blk", None),) * 2 + (P(),) * 15,
        check_vma=False,
    )
```

```python
import functools

import jax
import jax.numpy as jnp
from jax import lax
from jax.experimental import pallas as pl
from jax.experimental.pallas import tpu as pltpu
from jax.sharding import PartitionSpec as P

BIG = 1e30
VMEM_MIB = {"ffn_bwd": 36, "place": 24}
BF = jnp.bfloat16
F32 = jnp.float32


def matmul(left, right):
    return jnp.dot(left, right, preferred_element_type=F32)


def dot_nt(left, right):
    return lax.dot_general(left, right, (((1,), (1,)), ((), ())), preferred_element_type=F32)


def dot_tn(left, right):
    return lax.dot_general(left, right, (((0,), (0,)), ((), ())), preferred_element_type=F32)


def gelu_pair(x):
    mag = jnp.abs(x)
    bell = jnp.exp(-0.5 * x * x)
    t = 1.0 / (1.0 + 0.23164189 * mag)
    poly = t * (0.127414796 + t * (-0.142248368 + t * (0.7107068705 + t * (-0.7265760135 + t * 0.5307027145))))
    tail = poly * bell
    cdf = jnp.where(x >= 0, 1.0 - tail, tail)
    return x * cdf, cdf + x * (bell * 0.3989422804)


def norm_parts(value):
    center = value - jnp.mean(value, axis=-1, keepdims=True)
    spread = jnp.mean(center * center, axis=-1, keepdims=True)
    inv = lax.rsqrt(spread + 1e-12)
    return center * inv, inv


def norm_back(grad, gain, unit, inv):
    scaled = grad * gain
    mean = jnp.mean(scaled, axis=-1, keepdims=True)
    along = jnp.mean(scaled * unit, axis=-1, keepdims=True)
    return inv * (scaled - mean - unit * along)


def call(kernel, grid, ins, outs, shapes, scratch=(), scalars=0, flops=0, moved=0, exps=0, name=None, aliases=None):
    limit = VMEM_MIB.get(name, 60) * 1024 * 1024
    return pl.pallas_call(
        kernel,
        grid_spec=pltpu.PrefetchScalarGridSpec(
            num_scalar_prefetch=scalars, grid=grid, in_specs=ins, out_specs=outs, scratch_shapes=list(scratch)
        ),
        out_shape=[jax.ShapeDtypeStruct(s, d) for s, d in shapes],
        compiler_params=pltpu.CompilerParams(vmem_limit_bytes=limit),
        cost_estimate=pl.CostEstimate(flops=int(flops), bytes_accessed=int(moved), transcendentals=int(exps)),
        input_output_aliases=aliases or {},
        name=name,
    )


def whole(*shape):
    return pl.BlockSpec(shape, lambda *_: (0,) * len(shape))


def column_sum(value):
    return jnp.sum(value, axis=0, keepdims=True)


def attn_fwd_kernel(*refs, row, pieces):
    parts, refs = refs[:pieces], refs[pieces:]
    wq_ref, wk_ref, wv_ref, wo_ref, bq_ref, bv_ref, bo_ref, e_ref, f_ref = refs[:9]
    x_ref, unit_ref, inv_ref, *outs = refs[-16:-7]
    bufs, sems = refs[-7:-1], refs[-1]
    q_buf, k_buf, v_buf, ctx_buf, rb_buf, p_buf = bufs
    x = jnp.concatenate([part[0] for part in parts], axis=0)
    x_ref[0] = x
    e, f = e_ref[0], f_ref[0]
    heads = x.shape[1] // 64
    lo = lax.broadcasted_iota(jnp.int32, (1, 128), 1) < 64
    q = (matmul(x, wq_ref[...]) + bq_ref[...].astype(F32)).astype(BF) * BF(0.125)
    k = matmul(x, wk_ref[...]).astype(BF)
    v = (matmul(x, wv_ref[...]) + bv_ref[...].astype(F32)).astype(BF)

    def send(n):
        return pltpu.make_async_copy(bufs[n], outs[n].at[row], sems.at[n])

    def send_p(h):
        return pltpu.make_async_copy(p_buf.at[h], outs[5].at[row, h], sems.at[5 + h])

    q_buf[...], k_buf[...], v_buf[...] = q, k, v
    for n in range(3):
        send(n).start()
    for p in range(heads // 2):
        cut = slice(p * 128, (p + 1) * 128)
        qp, kp, vp = q[:, cut], k[:, cut], v[:, cut]
        raw = []
        for h in range(2):
            mine = ~lo if h else lo
            qa = jnp.where(mine, qp, e)
            ka = jnp.where(mine, kp, f)
            va = jnp.where(mine, vp, BF(1.0))
            s = dot_nt(qa, ka)
            w = jnp.exp(s - jnp.max(s, axis=-1, keepdims=True)).astype(BF)
            p_buf[2 * p + h] = w
            send_p(2 * p + h).start()
            raw.append(matmul(w, va))
        total = pltpu.roll(jnp.where(lo, raw[1], raw[0]), 64, 1)
        rb = 1.0 / total
        rb_buf[:, cut] = rb
        ctx_buf[:, cut] = (jnp.where(lo, raw[0], raw[1]) * rb).astype(BF)
    send(3).start()
    send(4).start()
    z = x.astype(F32) + bo_ref[...].astype(F32) + matmul(ctx_buf[...], wo_ref[...])
    unit, inv = norm_parts(z)
    unit_ref[0] = unit
    inv_ref[0] = jnp.broadcast_to(inv, inv_ref.shape[1:])
    for n in range(5):
        send(n).wait()
    for h in range(heads):
        send_p(h).wait()


def attn_forward(parts, row, rows, wq, wk, wv, wo, bq, bv, bo, e, f, before):
    seq, model = parts[0].shape[1] * len(parts), parts[0].shape[2]
    heads = model // 64
    full = pl.BlockSpec((1, seq, model), lambda i: (row, 0, 0))
    mask = pl.BlockSpec((1, seq, 128), lambda i: (row, 0, 0))
    far = pl.BlockSpec(memory_space=pl.ANY)
    big, sq = (rows, seq, model), (rows, heads, seq, seq)
    w, b = whole(model, model), whole(1, model)
    first = len(parts) + 9
    return call(
        functools.partial(attn_fwd_kernel, row=row, pieces=len(parts)),
        (1,),
        [whole(*parts[0].shape)] * len(parts) + [w, w, w, w, b, b, b, mask, mask] + [far] * len(before),
        [full, full, mask] + [far] * 6,
        [(big, BF), (big, F32), ((rows, seq, 128), F32)] + [(big, BF)] * 4 + [(big, F32), (sq, BF)],
        [pltpu.VMEM(big[1:], BF)] * 4
        + [pltpu.VMEM(big[1:], F32), pltpu.VMEM(sq[1:], BF), pltpu.SemaphoreType.DMA((5 + heads,))],
        flops=seq * model * (8 * model + 8 * seq),
        moved=seq * (model * 16 + heads * seq * 2) + 8 * model * model,
        exps=heads * seq * seq,
        name="attn_fwd",
        aliases={first + n: n for n in range(9)} if before else None,
    )(*parts, wq, wk, wv, wo, bq, bv, bo, e, f, *before)


def ffn_fwd_kernel(unit_ref, w1_ref, c1_ref, w2_ref, c2_ref, g1_ref, e1_ref, y1_ref, gel_ref, slope_ref, acc, *, chunk):
    i = pl.program_id(0)
    count = unit_ref.shape[0]

    @pl.when(i == 0)
    def _():
        y1 = unit_ref[...] * g1_ref[...].astype(F32) + e1_ref[...].astype(F32)
        y1_ref[...] = y1.astype(BF)
        acc[...] = y1 + c2_ref[...].astype(F32)

    c1 = c1_ref[...].astype(F32)
    for c in range(0, count, chunk):
        cut = slice(c, c + chunk)
        hidden = matmul(y1_ref[cut], w1_ref[...]) + c1
        gel, slope = gelu_pair(hidden)
        gel = gel.astype(BF)
        gel_ref[cut] = gel
        slope_ref[cut] = slope.astype(BF)
        acc[cut] += matmul(gel, w2_ref[...])


def ffn_forward(unit, w1, c1, w2, c2, g1, e1, tile=768, chunk=512):
    count, model = unit.shape
    ff = w1.shape[1]
    full, b = whole(count, model), whole(1, model)
    cols = pl.BlockSpec((count, tile), lambda i: (0, i))
    return call(
        functools.partial(ffn_fwd_kernel, chunk=chunk),
        (ff // tile,),
        [
            full, pl.BlockSpec((model, tile), lambda i: (0, i)), pl.BlockSpec((1, tile), lambda i: (0, i)),
            pl.BlockSpec((tile, model), lambda i: (i, 0)), b, b, b,
        ],
        [full, cols, cols, full],
        [((count, model), BF), ((count, ff), BF), ((count, ff), BF), ((count, model), F32)],
        flops=4 * count * model * ff,
        moved=4 * model * ff + 4 * count * ff + 12 * count * model,
        exps=count * ff,
        name="ffn_fwd",
    )(unit, w1, c1, w2, c2, g1, e1)


def last_norm_kernel(z_ref, *refs):
    parts = refs[:-5]
    g2_ref, e2_ref, out_ref, dff_ref, sums_ref = refs[-5:]
    i = pl.program_id(0)
    g2 = g2_ref[...].astype(F32)
    rows, width, model = z_ref.shape
    unit, inv = norm_parts(z_ref[...].reshape(rows * width, model))
    out_ref[...] = (unit * g2 + e2_ref[...].astype(F32)).astype(BF).reshape(1, rows, width, model)

    @pl.when(i == 0)
    def _():
        sums_ref[...] = jnp.zeros_like(sums_ref)

    for n, part in enumerate(parts):

        @pl.when(i == n)
        def _(part=part):
            g = part[...].reshape(rows * width, model).astype(F32)
            dff = norm_back(g, g2, unit, inv).astype(BF)
            dff_ref[...] = dff.reshape(rows, width, model)
            for m, item in enumerate((g * unit, g, dff.astype(F32))):
                sums_ref[m : m + 1] += column_sum(item)


def last_norm(z, parts, g2, e2):
    rows, width, model = parts[0].shape
    block = pl.BlockSpec((rows, width, model), lambda i: (0, i, 0))
    return call(
        last_norm_kernel,
        (len(parts),),
        [block] + [whole(rows, width, model)] * len(parts) + [whole(1, model)] * 2,
        [pl.BlockSpec((1, rows, width, model), lambda i: (i, 0, 0, 0)), block, whole(8, model)],
        [((len(parts), rows, width, model), BF), (z.shape, BF), ((8, model), F32)],
        moved=10 * z.size,
        name="last_norm",
    )(z, *parts, g2, e2)


def grad_w2_kernel(half_ref, gel_ref, dff_ref, out_ref):
    out_ref[...] = dot_tn(gel_ref[...], dff_ref[...]).astype(BF)


def grad_w2_half(which, gel, dff, tile=768):
    count, ff = gel.shape
    model = dff.shape[1]
    half = ff // tile // 2
    return call(
        grad_w2_kernel,
        (half,),
        [pl.BlockSpec((count, tile), lambda i, m: (0, i + half * m[0])), whole(count, model)],
        [pl.BlockSpec((tile, model), lambda i, m: (i, 0))],
        [((ff // 2, model), BF)],
        scalars=1,
        flops=count * model * ff,
        moved=count * ff + ff * model,
        name="grad_w2",
    )(which, gel, dff)[0]


def ffn_bwd_kernel(core_ref, dff_ref, w2_ref, slope_ref, w1_ref, ys_ref, yk_ref, start_ref, *rest, chunk):
    send_ref, keep_ref, acc, c1_ref, dh_buf = rest[-5:]
    i = pl.program_id(0)
    count = dff_ref.shape[0]

    @pl.when(i == 0)
    def _():
        acc[...] = start_ref[...].astype(F32)

    total = None
    for c in range(0, count, chunk):
        cut = slice(c, c + chunk)
        dh = (dot_nt(dff_ref[cut], w2_ref[...]) * slope_ref[cut].astype(F32)).astype(BF)
        dh_buf[cut] = dh
        got = column_sum(dh.astype(F32))
        total = got if total is None else total + got
        acc[cut] += dot_nt(dh, w1_ref[...])
    c1_ref[pl.ds(i, 1)] = total
    dh = dh_buf[...]
    send_ref[...] = dot_tn(ys_ref[...], dh).astype(BF)
    keep_ref[...] = dot_tn(yk_ref[...], dh).astype(BF)


def ffn_backward(core, dff, w2, slope, w1, y1, start, grads, part, parts, chunk=256, tile=768):
    count, model = dff.shape
    ff = w1.shape[1]
    half = model // 2
    n = ff // tile // parts
    full = whole(count, model)
    out = pl.BlockSpec((half, tile), lambda i, m: (0, i + n * part))
    return call(
        functools.partial(ffn_bwd_kernel, chunk=chunk),
        (n,),
        [
            full, pl.BlockSpec((tile, model), lambda i, m: (i + n * part, 0)),
            pl.BlockSpec((count, tile), lambda i, m: (0, i + n * part)),
            pl.BlockSpec((model, tile), lambda i, m: (0, i + n * part)),
            pl.BlockSpec((count, half), lambda i, m: (0, 1 - m[0])), pl.BlockSpec((count, half), lambda i, m: (0, m[0])),
            full,
        ]
        + [pl.BlockSpec(memory_space=pl.ANY)] * len(grads),
        [out, out, full, whole(8, tile)],
        [((half, ff), BF)] * 2 + [((count, model), F32), ((8, tile), F32)],
        [pltpu.VMEM((count, tile), BF)],
        scalars=1,
        flops=6 * count * model * ff // parts,
        moved=(6 * model * ff + 2 * count * ff) // parts + 8 * count * model,
        name="ffn_bwd",
        aliases={8: 0, 9: 1} if grads else None,
    )(core, dff, w2, slope, w1, y1, y1, start, *grads)


def norm_bwd_kernel(
    core_ref, dy_ref, unit_ref, inv_ref, g1_ref, cs_ref, ck_ref, wo_ref,
    send_ref, keep_ref, dctx_ref, da_ref, sums_ref, acc_s, acc_k,
):
    i = pl.program_id(0)
    dy, unit = dy_ref[...], unit_ref[...]
    da = norm_back(dy, g1_ref[...].astype(F32), unit, inv_ref[:, 0:1]).astype(BF)
    da_ref[...] = da
    dctx_ref[...] = dot_nt(da, wo_ref[...]).astype(BF)

    @pl.when(i == 0)
    def _():
        acc_s[...] = jnp.zeros_like(acc_s)
        acc_k[...] = jnp.zeros_like(acc_k)
        sums_ref[...] = jnp.zeros_like(sums_ref)

    acc_s[...] += dot_tn(cs_ref[...], da)
    acc_k[...] += dot_tn(ck_ref[...], da)
    for n, item in enumerate((dy * unit, dy, da.astype(F32))):
        sums_ref[n : n + 1] += column_sum(item)

    @pl.when(i == pl.num_programs(0) - 1)
    def _():
        for n in range(send_ref.shape[0]):
            cut = slice(n * 256, (n + 1) * 256)
            send_ref[n] = acc_s[:, cut].astype(BF)
            keep_ref[n] = acc_k[:, cut].astype(BF)


def norm_backward(core, dy, unit, inv, g1, ctx, wo, tile=256):
    count, model = dy.shape
    half = model // 2
    part = pl.BlockSpec((tile, model), lambda i, m: (i, 0))
    out = pl.BlockSpec((model // 256, half, 256), lambda i, m: (0, 0, 0))
    return call(
        norm_bwd_kernel,
        (count // tile,),
        [
            part, part, pl.BlockSpec((tile, 128), lambda i, m: (i, 0)), whole(1, model),
            pl.BlockSpec((tile, half), lambda i, m: (i, 1 - m[0])), pl.BlockSpec((tile, half), lambda i, m: (i, m[0])),
            whole(model, model),
        ],
        [out, out, part, part, whole(8, model)],
        [((4 * model // 256, half, 256), BF)] * 2 + [((count, model), BF)] * 2 + [((8, model), F32)],
        [pltpu.VMEM((half, model), F32)] * 2,
        scalars=1,
        flops=4 * count * model * model,
        moved=16 * count * model + 4 * model * model,
        name="norm_bwd",
    )(core, dy, unit, inv, g1, ctx, ctx, wo)


def attn_bwd_kernel(
    core_ref, p_ref, q_ref, k_ref, v_ref, dctx_ref, ctx_ref, rb_ref, xs_ref, xk_ref, *rest
):
    send_ref, keep_ref, dq_ref, dk_ref, dv_ref, sums_ref, acc_s, acc_k = rest[-8:]
    r = pl.program_id(0)
    last = pl.num_programs(0) - 1
    lane = lax.broadcasted_iota(jnp.int32, (1, 128), 1)
    lo = lane < 64
    zero = BF(0.0)
    grads = ([], [], [])
    for p in range(q_ref.shape[2] // 128):
        cut = slice(p * 128, (p + 1) * 128)
        q, k, v = q_ref[0, :, cut], k_ref[0, :, cut], v_ref[0, :, cut]
        scaled = dctx_ref[0, :, cut].astype(F32) * rb_ref[0, :, cut]
        da = scaled.astype(BF)
        prod = scaled * ctx_ref[0, :, cut].astype(F32)
        got = ([], [], [])
        for h in range(2):
            mine = ~lo if h else lo
            other = 0 if h else 64
            delta = jnp.sum(jnp.where(mine, prod, 0.0), axis=-1, keepdims=True)
            hi = delta.astype(BF)
            low = (delta - hi.astype(F32)).astype(BF)
            left = jnp.where(mine, da, jnp.where(lane == other, hi, jnp.where(lane == other + 1, low, zero)))
            right = jnp.where(mine, v, jnp.where((lane == other) | (lane == other + 1), BF(-1.0), zero))
            w = p_ref[0, 2 * p + h]
            ds = (w.astype(F32) * dot_nt(left, right)).astype(BF)
            got[0].append(matmul(ds, k))
            got[1].append(dot_tn(ds, q))
            got[2].append(dot_tn(w, da))
        for n in range(3):
            item = jnp.where(lo, got[n][0], got[n][1])
            grads[n].append((item * 0.125 if n == 0 else item).astype(BF))

    @pl.when(r == 0)
    def _():
        acc_s[...] = jnp.zeros_like(acc_s)
        acc_k[...] = jnp.zeros_like(acc_k)
        sums_ref[...] = jnp.zeros_like(sums_ref)

    for n, (items, ref) in enumerate(zip(grads, (dq_ref, dk_ref, dv_ref))):
        item = jnp.concatenate(items, axis=1)
        ref[0] = item
        acc_s[n] += dot_tn(xs_ref[0], item)
        acc_k[n] += dot_tn(xk_ref[0], item)
        if n != 1:
            at = n // 2
            sums_ref[at : at + 1] += column_sum(item.astype(F32))

    @pl.when(r == last)
    def _():
        send_ref[...] = acc_s[...].astype(BF)
        keep_ref[...] = acc_k[...].astype(BF)


def attn_backward(core, quad, p, q, k, v, dctx, ctx, rb, x, grads):
    rows, seq, model = x.shape
    wide = 256
    half = model // 2
    part = pl.BlockSpec((1, seq, wide), lambda r, m: (r, 0, quad))
    out = pl.BlockSpec((1, seq, wide), lambda r, m: (r, 0, 0))
    grad = pl.BlockSpec((3, half, wide), lambda r, m: (quad + 1, 0, 0))
    return call(
        attn_bwd_kernel,
        (rows,),
        [pl.BlockSpec((1, wide // 64, seq, seq), lambda r, m: (r, quad, 0, 0))]
        + [part] * 6
        + [
            pl.BlockSpec((1, seq, half), lambda r, m: (r, 0, 1 - m[0])),
            pl.BlockSpec((1, seq, half), lambda r, m: (r, 0, m[0])),
        ]
        + [pl.BlockSpec(memory_space=pl.ANY)] * len(grads),
        [grad, grad, out, out, out, whole(8, wide)],
        [(grads[0].shape, BF)] * 2 + [((rows, seq, wide), BF)] * 3 + [((8, wide), F32)],
        [pltpu.VMEM((3, half, wide), F32)] * 2,
        scalars=1,
        flops=rows * seq * wide * (6 * model + 16 * seq),
        moved=rows * seq * (wide * 30 + model * 2) + 6 * model * wide,
        name="attn_bwd",
        aliases={10: 0, 11: 1},
    )(core, p, q, k, v, dctx, ctx, rb, x, x, *grads)


def dx_kernel(da_ref, wq_ref, wk_ref, wv_ref, *rest):
    out_ref = rest[-1]
    total = da_ref[...].astype(F32)
    rows, width, model = total.shape
    total = total.reshape(rows * width, model)
    for n, w_ref in enumerate((wq_ref, wk_ref, wv_ref)):
        for c in range(model // 256):
            item = rest[3 * c + n][...].reshape(rows * width, 256)
            total += dot_nt(item, w_ref[:, c * 256 : (c + 1) * 256])
    out_ref[0] = total.reshape(rows, width, model).astype(BF)


def grad_x(da, wq, wk, wv, parts, width):
    rows, seq, model = da.shape
    block = lambda cols: pl.BlockSpec((rows, width, cols), lambda j: (0, j, 0))
    return call(
        dx_kernel,
        (seq // width,),
        [block(model)] + [whole(model, model)] * 3 + [block(256)] * len(parts),
        [pl.BlockSpec((1, rows, width, model), lambda j: (j, 0, 0, 0))],
        [((seq // width, rows, width, model), BF)],
        flops=6 * rows * seq * model * model,
        moved=10 * rows * seq * model + 6 * model * model,
        name="grad_x",
    )(da, wq, wk, wv, *parts)[0]


def hold(*items):
    return lax.optimization_barrier(items)


def swap(value, axis, mask):
    return lax.ppermute(value, axis, [(i, i ^ mask) for i in range(lax.axis_size(axis))])


def add(*items):
    if len(items) == 1:
        return items[0]
    total = items[0].astype(F32)
    for item in items[1:]:
        total = total + item.astype(F32)
    return total.astype(items[0].dtype)


def swap_by(value, partner):
    wide, blk = lax.axis_size("wide"), lax.axis_size("blk")
    pairs = []
    for i in range(wide * blk):
        w, b = partner(i // blk, i % blk)
        pairs.append((i, w * blk + b))
    return lax.ppermute(value, ("wide", "blk"), pairs)


def side(w, b):
    return w, b ^ 1


def first_hop(w, b):
    return (w, b ^ 2) if b & 1 else (w ^ 1, b)


def second_hop(w, b):
    return (w ^ 1, b) if b & 1 else (w, b ^ 2)


PAIRED = (side, first_hop, second_hop)


def bits_of_device():
    w, b = lax.axis_index("wide"), lax.axis_index("blk")
    core, x, y = b & 1, w & 1, (b >> 1) & 1
    odd = core == 1
    return core, jnp.where(odd, y, x), jnp.where(odd, x, y), (w >> 1) & 3


class Sum:
    stages = 8

    def __init__(self, send, keep, pairs=False):
        self.send, self.terms = send, [keep]
        self.pairs = pairs
        self.stage = 0
        self.flying = None

    def piece(self, at, size):
        axis = self.terms[0].ndim - 2
        return add(*[lax.dynamic_slice_in_dim(item, at * size, size, axis) for item in self.terms])

    def start(self):
        s = self.stage
        rows = self.terms[0].shape[-2] if s else 0
        bits = bits_of_device()
        hops = [lambda w, b, k=k: (w ^ (2 * k), b) for k in range(1, 4)]
        if s == 0:
            self.flying = [swap_by(self.send, side)]
        elif s < 3:
            self.flying = [swap_by(self.piece(1 - bits[s], rows // 2), PAIRED[s])]
            self.terms = [self.piece(bits[s], rows // 2)]
        elif self.pairs and s < 5:
            self.terms = [add(*self.terms)]
            self.flying = [swap(self.terms[0], "wide", 2 if s == 3 else 4)]
        elif s == 3:
            self.flying = [swap_by(self.piece(bits[3] ^ k, rows // 4), hops[k - 1]) for k in range(1, 4)]
            self.terms = [self.piece(bits[3], rows // 4)]
        elif s == 4:
            self.spread()
            self.flying = [swap_by(self.terms[0], hop) for hop in hops]
        else:
            if self.pairs and s == 5:
                self.spread()
            self.flying = [swap_by(self.terms[0], PAIRED[7 - s])]

    def spread(self):
        value = add(*self.terms)
        for i in range(3, lax.axis_size("wide").bit_length() - 1):
            value = add(value, swap(value, "wide", 1 << i))
        self.terms = [value]

    def finish(self):
        self.terms = self.terms + self.flying
        if (5 if self.pairs else 4) <= self.stage < 7:
            self.terms = [jnp.concatenate(self.terms, axis=self.terms[0].ndim - 2)]
        self.flying = None
        self.stage += 1


class SmallSum:
    def __init__(self, value):
        self.value = value
        self.stage = 0
        self.pairs = [(axis, 1 << i) for axis in ("blk", "wide") for i in range(lax.axis_size(axis).bit_length() - 1)]
        self.stages = len(self.pairs)

    def start(self):
        self.flying = [swap(self.value, *self.pairs[self.stage])]

    def finish(self):
        self.value = self.value + self.flying[0]
        self.stage += 1


def step(sums, held, compute=None):
    sums = [item for item in sums if item.stage < item.stages]
    for item in sums:
        item.start()
    flying = [item.flying for item in sums]
    flying, held = hold(flying, compute(*held) if compute else held)
    for item, got in zip(sums, flying):
        item.flying = got
        item.finish()
    return held


def place_kernel(me_ref, *refs, takes, pieces, ordered):
    outs = refs[2 * len(takes) :]
    low = 0 if ordered else me_ref[3]
    i = pl.program_id(0)
    for turn, when in enumerate((i < 4, i >= 4)):

        @pl.when(when)
        def _(turn=turn):
            for n, cuts in enumerate(takes):
                value_ref = refs[2 * n + turn]
                for out, lead, r, rows, a, b, width in cuts:
                    value = (value_ref[...] if lead is None else value_ref[lead]).astype(F32)
                    for k in range(4):
                        at = k * rows if ordered else pl.multiple_of((k ^ low) * rows, 8)
                        top = k * pieces[n] + r
                        outs[out][pl.ds(at, rows), b : b + width] = value[top : top + rows, a : a + width]


def place(pairs, takes, shapes, ordered=False):
    core, first, second, low = bits_of_device()
    me = jnp.stack([core, first * 2 + second, second * 2 + first, low]).astype(jnp.int32)

    def own_at(i, m):
        return jnp.minimum(i, 3) ^ m[1]

    def other_at(i, m):
        return jnp.maximum(i - 4, 0) ^ m[2]

    ins = []
    for own, _ in pairs:
        lead, group, cols = own.shape[:-2], own.shape[-2] // 4, own.shape[-1]
        for at in (own_at, other_at):
            if lead:
                ins.append(pl.BlockSpec((*lead, group, cols), lambda i, m, at=at: (0, at(i, m), 0)))
            else:
                ins.append(pl.BlockSpec((group, cols), lambda i, m, at=at: (at(i, m), 0)))
    out_at = lambda i, m: (jnp.where(i < 4, m[0] * 4 + i, (1 - m[0]) * 4 + i - 4), 0)
    return call(
        functools.partial(place_kernel, takes=takes, pieces=[own.shape[-2] // 16 for own, _ in pairs], ordered=ordered),
        (8,),
        ins,
        [pl.BlockSpec((rows // 8, cols), out_at) for rows, cols in shapes],
        [(shape, F32) for shape in shapes],
        scalars=1,
        moved=6 * sum(rows * cols for rows, cols in shapes),
        name="place",
    )(me, *[item for pair in pairs for item in pair])


def to_rows(value, first, count):
    parts = lax.axis_size("blk")
    own = value.shape[0] // parts
    me = lax.axis_index("blk")
    got = {}
    for j in reversed(range(parts)):
        piece = lax.dynamic_slice_in_dim(value, (me ^ j) * own + first, count, 0)
        got[j] = swap(piece, "blk", j) if j else piece
    return [got[j] for j in range(parts)]


def send_back(pieces):
    return [swap(pieces[j], "blk", j) if j else pieces[0] for j in range(lax.axis_size("blk"))]


def tokens_of(got):
    own, width, model = got[0].shape
    me = lax.axis_index("blk")
    out = jnp.zeros((own * len(got), width, model), got[0].dtype)
    for j, piece in enumerate(got):
        out = lax.dynamic_update_slice_in_dim(out, piece, (me ^ j) * own, 0)
    return out


def mask_lanes(lengths, own, width):
    parts = lax.axis_size("blk")
    me = lax.axis_index("blk")
    mine = lax.dynamic_slice_in_dim(lengths, me * own, own, 0)
    ends = jnp.cumsum(mine, axis=-1)
    start = (me ^ jnp.arange(parts, dtype=jnp.int32)) * width
    place_of = (start[:, None] + jnp.arange(width, dtype=jnp.int32)[None, :]).reshape(-1)
    seg = jnp.sum((place_of[None, :, None] >= ends[:, None, :]).astype(jnp.int32), axis=-1)
    lane = jnp.arange(128, dtype=jnp.int32) % 64
    same = seg[:, :, None] == lane
    docs = lane < 8
    e = jnp.where(same & docs, 1.0, 0.0).astype(BF)
    f = jnp.where(docs & ~same, -BIG, 0.0).astype(BF)
    return e, f


def per_device(
    tokens,
    lengths,
    query_weight,
    query_bias,
    key_weight,
    value_weight,
    value_bias,
    out_weight,
    out_bias,
    first_gain,
    first_shift,
    inner_weight,
    inner_bias,
    outer_weight,
    outer_bias,
    second_gain,
    second_shift,
    cotangent,
):
    rows_dev, width, model = tokens.shape
    parts = lax.axis_size("blk")
    rows, seq = rows_dev // parts, parts * width
    count = rows * seq
    shape3 = (rows, seq, model)
    flat = lambda item: item.reshape(count, item.shape[-1])
    line = lambda item: item.reshape(1, -1)
    bq, bv, bo, c1, c2 = map(line, (query_bias, value_bias, out_bias, inner_bias, outer_bias))
    g1, e1, g2, e2 = map(line, (first_gain, first_shift, second_gain, second_shift))
    core = (lax.axis_index("blk") & 1).reshape(1).astype(jnp.int32)

    e, f = mask_lanes(lengths, rows, width)
    got, e, f, tokens = hold(to_rows(tokens, 0, 1), e, f, tokens)
    before = []
    for r in range(rows):
        later = to_rows(tokens, r + 1, 1) if r + 1 < rows else to_rows(cotangent, 0, rows)
        before = attn_forward(
            got, r, rows, query_weight, key_weight, value_weight, out_weight, bq, bv, bo, e, f, before
        )
        if r + 1 < rows:
            got, before, cotangent = hold(later, before, cotangent)
    x, unit, inv, q, k, v, ctx, rb, p = before
    y1, gel, slope, z2 = ffn_forward(flat(unit), inner_weight, c1, outer_weight, c2, g1, e1)
    z2, pull = hold(z2, later)
    output, dff, sums_2 = last_norm(z2.reshape(shape3), pull, g2, e2)
    dff = flat(dff)
    back = send_back(output)
    send = grad_w2_half(1 - core, gel, dff)
    sum2 = Sum(*hold(send, core))
    sum2.start()
    sum2.flying, back[:3], keep = hold(sum2.flying, back[:3], grad_w2_half(sum2.terms[0], gel, dff))
    sum2.terms = [keep]
    sum2.finish()
    ff = inner_weight.shape[1]
    dy, grads, grad_c1 = dff, [], []
    for n in range(2):
        *grads, dy, got = step(
            [sum2],
            [dff, dy, grads],
            lambda dff, dy, grads: ffn_backward(
                core, dff, outer_weight, slope, inner_weight, y1, dy, grads, n, 2
            ),
        )
        grad_c1.append(got)
    sum1 = Sum(*grads)
    (*grads, dctx, da, sums_1), back[3:] = step(
        [sum2, sum1],
        [dy, back[3:]],
        lambda dy, back: (norm_backward(core, dy, flat(unit), flat(inv), g1, flat(ctx), out_weight), back),
    )
    output = tokens_of(back)
    dctx = dctx.reshape(shape3)
    bias, grads_x = [], []
    quads = model // 256
    for n in range(quads):
        (*grads, dq, dk, dv, got), output = step(
            [sum2, sum1],
            [dctx, grads, output],
            lambda dctx, grads, output: (attn_backward(core, n, p, q, k, v, dctx, ctx, rb, x, grads), output),
        )
        bias.append(got)
        grads_x += [dq, dk, dv]
    sum3 = Sum(*grads)
    tall, broad = ff // 32, model // 32
    sum1.start()
    bias = jnp.concatenate([item[:2] for item in bias], axis=1)
    small = jnp.concatenate([bias, sums_1[:3], sums_2[:3]] + [item[: ff // model // 2] for item in grad_c1], axis=0)
    sum2.terms, small = step([sum3], [sum2.terms, small])
    joined = SmallSum(small)
    (dx,) = step(
        [sum3, sum2, joined],
        [grads_x],
        lambda parts: [grad_x(da.reshape(shape3), query_weight, key_weight, value_weight, parts, width)],
    )
    back = [dx[0], swap(dx[1], "blk", 1)]
    back, dx = step([sum3, joined], [back, dx])
    (sum1.flying,) = hold(sum1.flying)
    sum1.finish()
    back.append(swap(dx[2], "blk", 2))
    back, dx = step([sum3, sum1], [back, dx])
    back.append(swap(dx[3], "blk", 3))
    (grad_w2,), back = step(
        [sum3, sum1],
        [sum2.terms, back],
        lambda value, back: (place([value], [[(0, None, 0, tall, 0, 0, model)]], [(ff, model)]), back),
    )
    grad_tokens = tokens_of(back)
    grad_tokens, sum1.terms = step([sum3, joined], [grad_tokens, sum1.terms])
    step([sum3, sum1, joined], [])
    (grad_w1,) = step(
        [sum3, joined],
        [sum1.terms],
        lambda value: place([value], [[(0, None, 0, broad, 0, 0, ff)]], [(model, ff)]),
    )
    sums = [joined.value[n] for n in range(8)] + [joined.value[8:].reshape(-1)]
    takes = [(n, 3 + 3 * c + n, 0, broad, 0, 256 * c, 256) for c in range(quads) for n in range(3)]
    takes += [(3, c, 0, broad, 0, 256 * c, 256) for c in range(quads)]
    grad_wq, grad_wk, grad_wv, grad_wo = place([sum3.terms], [takes], [(model, model)] * 4)
    grad_bq, grad_bv, grad_g1, grad_e1, grad_bo, grad_g2, grad_e2, grad_c2, grad_c1 = sums
    return (
        output,
        grad_tokens,
        grad_wq,
        grad_bq,
        grad_wk,
        grad_wv,
        grad_bv,
        grad_wo,
        grad_bo,
        grad_g1,
        grad_e1,
        grad_w1,
        grad_c1,
        grad_w2,
        grad_c2,
        grad_g2,
        grad_e2,
    )


def solution(mesh):
    placed = (P("wide", "blk", None), P("wide", None)) + (P(),) * 15 + (P("wide", "blk", None),)
    return jax.shard_map(
        per_device,
        mesh=mesh,
        in_specs=placed,
        out_specs=(P("wide", "blk", None),) * 2 + (P(),) * 15,
        check_vma=False,
    )
```
